32 devices in a mesh: fy: 8 (over y, x, core), fx: 4 (over z).
Axes of the slice: x: 2, y: 2, z: 4, core: 2. Of those that a mesh axis runs over, the one named last changes fastest.
Arguments:
- start_image: float32 [16, 256, 512], P(None, 'fy', 'fx'), may hold values from 0.2 to 2
- dirty: float32 [16, 256, 512], P(None, 'fy', 'fx'), may hold values from -50 to 50
- sampling: float32 [16, 256, 512], P(None, 'fy', 'fx'), may hold values from 0.25 to 1
- basis_seed: float32 [16, 4], replicated, may hold values from -0.75 to 2.75
- margin: int32 [8, 4, 2, 2], P('fy', 'fx'), may hold values from 8 to 30, as said below
Outputs:
- image: float32 [16, 256, 512], P(None, 'fy', 'fx')
- data_dual: float32 [16, 256, 512], P(None, 'fy', 'fx')
The draws below stay inside these ranges and needn't reach their ends.
Inputs may be any that keep to these rules, and one draw needn't show every extreme that they name: margin[a, b, l, 0] and margin[a, b, l, 1] are the widths kept above and to the left at dilation 2^l, at most 15 * 2^l; the value 30 occurs at the widest dilation in every draw.
All inputs are finite; a program needn't handle non-finite values.
Results may differ from the reference program's by a relative error of at most 0.0003.
Values sent between devices are 32-bit elements; how exact they have to be, the bound alone decides.
No kernel may reach another device: no remote copies, remote signals or barrier semaphores. Data moves between devices by JAX's collectives and lax.ppermute only.
A program may use at most 64 MiB of HBM per device.

```python
import math
from functools import partial
import jax
import jax.numpy as jnp
from jax import lax

C = 16
RANK = 4
TAPS = 16
LEVELS = 2
ITERS = 1
ROWS_DEV = 32
COLS_DEV = 128
NROWS = 256
NCOLS = 512


def draw_dirty(key, part):
    first, second, third = jax.random.split(key, 3)
    row_pos = jnp.arange(NROWS).astype(jnp.float32) / NROWS
    col_pos = jnp.arange(NCOLS).astype(jnp.float32) / NCOLS
    row_scale = jnp.exp(jax.random.uniform(second, (NROWS,), jnp.float32, 0.0, math.log(3.2))) * (1.0 + row_pos)
    col_scale = jnp.exp(jax.random.uniform(third, (NCOLS,), jnp.float32, 0.0, math.log(3.2))) * (1.0 + col_pos)
    base_field = jnp.clip(jax.random.normal(first, (C, NROWS, NCOLS), jnp.float32), -4.0, 4.0)
    return 0.3 * base_field * row_scale[None, :, None] * col_scale[None, None, :]


def draw_basis_seed(key, part):
    noise = jnp.clip(jax.random.normal(key, (C, RANK), jnp.float32), -3.0, 3.0) * 0.25
    leading = (jnp.arange(C)[:, None] % RANK == jnp.arange(RANK)[None, :]).astype(jnp.float32) * 2.0
    return noise + leading


def draw_margin(key, part):
    facet_rows = NROWS // ROWS_DEV
    facet_cols = NCOLS // COLS_DEV
    reach_level = (TAPS - 1) * 2 ** jnp.arange(LEVELS)
    first, second = jax.random.split(key, 2)
    raw_cut = jax.random.randint(first, (facet_rows, facet_cols, LEVELS, 2), 0, 1 << 20)
    cut_width = raw_cut % (reach_level // 2 + 1)[None, None, :, None]
    widths = reach_level[None, None, :, None] - cut_width
    chosen = jax.random.randint(second, (), 0, facet_rows * facet_cols)
    facet_ids = jnp.arange(facet_rows * facet_cols).reshape(facet_rows, facet_cols)
    level_ids = jnp.arange(LEVELS)
    target = (facet_ids == chosen)[:, :, None, None] & (level_ids == LEVELS - 1)[None, None, :, None]
    return jnp.where(target, reach_level[LEVELS - 1], widths).astype(jnp.int32)


def block_levels(own_key, shape, shards, least, high):
    gain, own = 1.0, jax.random.fold_in(own_key, 6)
    for axis_at, parts in shards:
        draws = jnp.exp(jax.random.uniform(jax.random.fold_in(own, axis_at), (parts,), jnp.float32, least / len(shards), high / len(shards)))
        gain = gain * jnp.repeat(draws, shape[axis_at] // parts).reshape([-1 if axis == axis_at else 1 for axis in range(len(shape))])
    return gain


def setup_inputs(seed: int = 0) -> dict:
    splits = jax.random.split(jax.random.key(seed), 6)
    return {
        "start_image": jnp.clip(jnp.exp(math.log(2.0) - 2.3025851 * jax.random.uniform(splits[0], (C, NROWS, NCOLS), jnp.float32) ** block_levels(splits[0], (C, NROWS, NCOLS), ((1, 8), (2, 4)), -0.2, 0.2)), 0.2, 2.0),
        "dirty": draw_dirty(jax.random.fold_in(splits[5], 71), 0),
        "sampling": jnp.clip(0.25 + 0.75 * jax.random.uniform(splits[2], (C, NROWS, NCOLS), jnp.float32) ** block_levels(splits[2], (C, NROWS, NCOLS), ((1, 8), (2, 4)), -0.2, 0.2), 0.25, 1.0),
        "basis_seed": draw_basis_seed(jax.random.fold_in(splits[5], 71), 0),
        "margin": draw_margin(jax.random.fold_in(splits[5], 71), 0),
    }


DAUBECHIES = [-0.00011747678400228192, 0.0006754494059985568, -0.0003917403729959771, -0.00487035299301066, 0.008746094047015655, 0.013981027917015516, -0.04408825393106472, -0.01736930100202211, 0.128747426620186, 0.00047248457399797254, -0.2840155429624281, -0.015829105256023893, 0.5853546836548691, 0.6756307362980128, 0.3128715909144659, 0.05441584224308161]
DUAL_STEP = 0.5
PRIMAL_STEP = 0.5
CLIP_LEVEL = 0.08
BALL_SCALE = 0.8
NORM_EPS = 1e-06

def band_matrix(filter_taps, extent, border, dilation):
    rows_idx = jnp.arange(extent + border)[:, None]
    cols_idx = jnp.arange(extent)[None, :]
    offset = cols_idx + border - rows_idx
    matrix = jnp.zeros((extent + border, extent), jnp.float32)
    for tap_idx in range(len(filter_taps)):
        matrix = matrix + filter_taps[tap_idx] * (offset == tap_idx * dilation).astype(jnp.float32)
    return matrix

def level_tables(row_count, col_count, border, dilation):
    low_taps = [tap_value / math.sqrt(2.0) for tap_value in DAUBECHIES]
    high_taps = [(-1.0) ** tap_idx * low_taps[len(low_taps) - 1 - tap_idx] for tap_idx in range(len(low_taps))]
    return (band_matrix(low_taps, row_count, border, dilation), band_matrix(high_taps, row_count, border, dilation), band_matrix(low_taps, col_count, border, dilation), band_matrix(high_taps, col_count, border, dilation))

def facet_mask(widths_pair, row_count, col_count, border):
    row_keep = (jnp.arange(row_count + border) >= border - widths_pair[0]).astype(jnp.float32)
    col_keep = (jnp.arange(col_count + border) >= border - widths_pair[1]).astype(jnp.float32)
    return row_keep[:, None] * col_keep[None, :]

def analyse(extended, tables):
    low_rows, high_rows, low_cols, high_cols = tables
    highest = lax.Precision.HIGHEST
    col_low = jnp.einsum('cjv,vw->cjw', extended, low_cols, precision=highest)
    col_high = jnp.einsum('cjv,vw->cjw', extended, high_cols, precision=highest)
    band_lh = jnp.einsum('ji,cjw->ciw', low_rows, col_high, precision=highest)
    band_hl = jnp.einsum('ji,cjw->ciw', high_rows, col_low, precision=highest)
    band_hh = jnp.einsum('ji,cjw->ciw', high_rows, col_high, precision=highest)
    return jnp.stack([band_lh, band_hl, band_hh])

def synthesise(bands, tables):
    low_rows, high_rows, low_cols, high_cols = tables
    highest = lax.Precision.HIGHEST
    rows_high = jnp.einsum('ji,ciw->cjw', low_rows, bands[0], precision=highest) + jnp.einsum('ji,ciw->cjw', high_rows, bands[2], precision=highest)
    rows_low = jnp.einsum('ji,ciw->cjw', high_rows, bands[1], precision=highest)
    return jnp.einsum('cjw,vw->cjv', rows_high, high_cols, precision=highest) + jnp.einsum('cjw,vw->cjv', rows_low, low_cols, precision=highest)

def orthonormal(basis_seed):
    columns = []
    for column_idx in range(basis_seed.shape[1]):
        vector = basis_seed[:, column_idx]
        for previous in columns:
            vector = vector - jnp.sum(previous * vector) * previous
        vector = vector / jnp.sqrt(jnp.sum(vector * vector))
        columns.append(vector)
    return jnp.stack(columns, axis=1)

def project(spectral, stepped):
    highest = lax.Precision.HIGHEST
    weights = jnp.einsum('cr,cij->rij', spectral, stepped, precision=highest)
    return jnp.einsum('cr,rij->cij', spectral, weights, precision=highest)

def to_tiles(field, facet_rows, facet_cols):
    channels = field.shape[0]
    return field.reshape(channels, facet_rows, ROWS_DEV, facet_cols, COLS_DEV).transpose(1, 3, 0, 2, 4)

def from_tiles(tiles):
    facet_rows, facet_cols, channels, row_count, col_count = tiles.shape
    return tiles.transpose(2, 0, 3, 1, 4).reshape(channels, facet_rows * row_count, facet_cols * col_count)

def extend_whole(tiles, border):
    from_above = jnp.concatenate([jnp.zeros_like(tiles[:1, :, :, -border:, :]), tiles[:-1, :, :, -border:, :]], axis=0)
    taller = jnp.concatenate([from_above, tiles], axis=3)
    from_left = jnp.concatenate([jnp.zeros_like(taller[:, :1, :, :, -border:]), taller[:, :-1, :, :, -border:]], axis=1)
    return jnp.concatenate([from_left, taller], axis=4)

def retract_whole(grown, border):
    border_strip = grown[..., :border]
    interior = grown[..., border:]
    arrived = jnp.concatenate([border_strip[:, 1:], jnp.zeros_like(border_strip[:, :1])], axis=1)
    interior = jnp.concatenate([interior[..., :-border], interior[..., -border:] + arrived], axis=4)
    border_strip = interior[:, :, :, :border, :]
    interior = interior[:, :, :, border:, :]
    arrived = jnp.concatenate([border_strip[1:], jnp.zeros_like(border_strip[:1])], axis=0)
    return jnp.concatenate([interior[:, :, :, :-border, :], interior[:, :, :, -border:, :] + arrived], axis=3)

def reference(start_image, dirty, sampling, basis_seed, margin):
    spectral = orthonormal(basis_seed)
    facet_rows = NROWS // ROWS_DEV
    facet_cols = NCOLS // COLS_DEV
    radius = BALL_SCALE * math.sqrt(C * NROWS * NCOLS)
    weight = 1.0 / math.sqrt(LEVELS)
    current = start_image
    relaxed = start_image
    data_dual = jnp.zeros_like(start_image)
    band_duals = [jnp.zeros((facet_rows, facet_cols, 3, C, ROWS_DEV, COLS_DEV), jnp.float32) for level_idx in range(LEVELS)]
    for iteration in range(ITERS):
        shifted = data_dual + DUAL_STEP * sampling * relaxed - DUAL_STEP * dirty
        energy = jnp.sum(shifted * shifted)
        factor = jnp.maximum(0.0, 1.0 - DUAL_STEP * radius / jnp.sqrt(energy + NORM_EPS))
        data_dual = factor * shifted
        relaxed_tiles = to_tiles(relaxed, facet_rows, facet_cols)
        prior_tiles = jnp.zeros_like(relaxed_tiles)
        for level_idx in range(LEVELS):
            dilation = 2 ** level_idx
            border = (TAPS - 1) * dilation
            tables = level_tables(ROWS_DEV, COLS_DEV, border, dilation)
            keep_mask = jax.vmap(jax.vmap(partial(facet_mask, row_count=ROWS_DEV, col_count=COLS_DEV, border=border)))(margin[:, :, level_idx, :])[:, :, None]
            extended = extend_whole(relaxed_tiles, border) * keep_mask
            coefficients = jax.vmap(jax.vmap(partial(analyse, tables=tables)))(extended)
            band_duals[level_idx] = jnp.clip(band_duals[level_idx] + DUAL_STEP * weight * coefficients, -CLIP_LEVEL, CLIP_LEVEL)
            returned = jax.vmap(jax.vmap(partial(synthesise, tables=tables)))(band_duals[level_idx]) * keep_mask
            prior_tiles = prior_tiles + retract_whole(returned, border)
        stepped = current - PRIMAL_STEP * (sampling * data_dual + weight * from_tiles(prior_tiles))
        updated = jnp.maximum(project(spectral, stepped), 0.0)
        relaxed = 2.0 * updated - current
        current = updated
    return (current, data_dual)
```

```python
import math

import jax
import jax.numpy as jnp
import numpy as np
from jax import lax
from jax.experimental import pallas as pl
from jax.experimental.pallas import tpu as pltpu
from jax.sharding import PartitionSpec as P

LEVELS = 2
BORDER = 32
LANES = 128


DAUBECHIES = [
    -0.00011747678400228192,
    0.0006754494059985568,
    -0.0003917403729959771,
    -0.00487035299301066,
    0.008746094047015655,
    0.013981027917015516,
    -0.04408825393106472,
    -0.01736930100202211,
    0.128747426620186,
    0.00047248457399797254,
    -0.2840155429624281,
    -0.015829105256023893,
    0.5853546836548691,
    0.6756307362980128,
    0.3128715909144659,
    0.05441584224308161,
]
DUAL_STEP = 0.5
PRIMAL_STEP = 0.5
CLIP_LEVEL = 0.08
BALL_SCALE = 0.8
NORM_EPS = 1e-06
WEIGHT = 1.0 / math.sqrt(LEVELS)
BAND_STEP = DUAL_STEP * WEIGHT

LOW = [tap / math.sqrt(2.0) for tap in DAUBECHIES]
HIGH = [(-1.0) ** k * LOW[len(LOW) - 1 - k] for k in range(len(LOW))]


def band(taps, extent, dilation):
    matrix = np.zeros((BORDER + extent, extent), np.float32)
    for k, tap in enumerate(taps):
        for i in range(extent):
            matrix[i - k * dilation + BORDER, i] += np.float32(tap)
    return matrix


def row_table(rows):
    return np.concatenate(
        [band(taps, rows, 2**level).T for level in range(LEVELS) for taps in (LOW, HIGH)], axis=0
    )


def col_table(cols):
    table = np.zeros((LEVELS, cols + LANES, 2 * cols), np.float32)
    for level in range(LEVELS):
        for half, taps in enumerate((LOW, HIGH)):
            matrix = band(taps, cols, 2**level)
            table[level, :cols, half * cols : (half + 1) * cols] = matrix[BORDER:]
            table[level, cols : cols + BORDER, half * cols : (half + 1) * cols] = matrix[:BORDER]
    return table


def terms(value):
    high = value.astype(jnp.bfloat16)
    low = (value - high.astype(jnp.float32)).astype(jnp.bfloat16)
    return high, low


def dot(a, b):
    return lax.dot_general(a, b, (((1,), (0,)), ((), ())), preferred_element_type=jnp.float32)


def lane_iota(shape):
    return lax.broadcasted_iota(jnp.int32, shape, len(shape) - 1)


def row_iota(shape):
    return lax.broadcasted_iota(jnp.int32, shape, len(shape) - 2)


def pack_rows(strip, offset):
    groups = strip.shape[0] // 8
    lane = lane_iota((8, LANES))
    packed = None
    for q in range(groups):
        piece = strip[8 * q : 8 * q + 8]
        shift = (BORDER * q - offset) % LANES
        if shift:
            piece = pltpu.roll(piece, shift, 1)
        packed = piece if packed is None else jnp.where(lane >= BORDER * q, piece, packed)
    return packed


def unpack_rows(packed, offset, groups):
    pieces = []
    for q in range(groups):
        shift = (offset - BORDER * q) % LANES
        pieces.append(pltpu.roll(packed, shift, 1) if shift else packed)
    return jnp.concatenate(pieces, axis=0)


def first_kernel(start_ref, dirty_ref, sampling_ref, energy_ref, pack_ref):
    channels, rows, cols = start_ref.shape
    total = jnp.zeros((8, cols), jnp.float32)
    for c in range(channels):
        field = start_ref[c]
        shifted = DUAL_STEP * sampling_ref[c] * field - DUAL_STEP * dirty_ref[c]
        square = shifted * shifted
        for q in range(rows // 8):
            total = total + square[8 * q : 8 * q + 8]
        pack_ref[c] = pack_rows(field, cols - BORDER)
    energy_ref[...] = total


def basis_kernel(seed_ref, basis_ref):
    channels, rank = seed_ref.shape
    seed = seed_ref[...]
    columns = [jnp.broadcast_to(seed[:, r : r + 1], (channels, LANES)) for r in range(rank)]
    for r in range(rank):
        vector = columns[r]
        vector = vector / jnp.sqrt(jnp.sum(vector * vector, axis=0, keepdims=True))
        basis_ref[r] = vector
        for later in range(r + 1, rank):
            along = jnp.sum(vector * columns[later], axis=0, keepdims=True)
            columns[later] = columns[later] - along * vector


def bank_kernel(
    margin_ref, own_ref, above_ref, left_ref, corner_ref, rows_ref, rows_t_ref, cols_ref, cols_t_ref,
    own_out, above_out, left_out, corner_out, z_high, z_low, u_high, u_low,
):
    channels, rows, cols = own_ref.shape
    groups = rows // 8
    tall = rows + BORDER
    wide = cols + LANES
    half = 2 * rows

    position = lane_iota((half, tall)) - BORDER
    position_t = row_iota((tall, half)) - BORDER
    a_parts, at_parts = [], []
    for level in range(LEVELS):
        width = margin_ref[2 * level]
        a_parts.append(jnp.where(position >= -width, rows_ref[level * half : (level + 1) * half], 0.0))
        at_parts.append(jnp.where(position_t >= -width, rows_t_ref[level], 0.0))
    a_high, a_low = terms(jnp.concatenate(a_parts, axis=0))
    a_cat = jnp.concatenate([a_high, a_high, a_low], axis=1)
    at_pairs = [terms(part) for part in at_parts]
    at_cat = jnp.concatenate(
        [pair[0] for pair in at_pairs] * 2 + [pair[1] for pair in at_pairs], axis=1
    )

    for c in range(channels):
        upper = jnp.concatenate([above_ref[c], unpack_rows(corner_ref[c], 0, groups)], axis=1)
        lower = jnp.concatenate([own_ref[c], unpack_rows(left_ref[c], 0, groups)], axis=1)
        e_high, e_low = terms(jnp.concatenate([upper, lower], axis=0))
        z = dot(a_cat, jnp.concatenate([e_high, e_low, e_high], axis=0))
        part_high, part_low = terms(z)
        for level in range(LEVELS):
            z_high[level, c] = part_high[level * half : (level + 1) * half]
            z_low[level, c] = part_low[level * half : (level + 1) * half]

    low_rows = row_iota((half, 2 * cols)) < rows
    low_cols = lane_iota((half, 2 * cols)) < cols
    bound = jnp.where(low_rows & low_cols, 0.0, CLIP_LEVEL / BAND_STEP)
    bound = jnp.broadcast_to(bound[None], (channels, half, 2 * cols)).reshape(channels * half, 2 * cols)
    for level in range(LEVELS):
        width = margin_ref[2 * level + 1]
        at = row_iota((wide, 2 * cols))
        g = jnp.where((at < cols) | (at >= cols + BORDER - width), cols_ref[level], 0.0)
        at = lane_iota((2 * cols, wide))
        g_t = jnp.where((at < cols) | (at >= cols + BORDER - width), cols_t_ref[level], 0.0)
        g_high, g_low = terms(g)
        zh = z_high[level].reshape(channels * half, wide)
        zl = z_low[level].reshape(channels * half, wide)
        coef = dot(jnp.concatenate([zh, zl, zh], axis=1), jnp.concatenate([g_high, g_high, g_low], axis=0))
        coef = jnp.minimum(jnp.maximum(coef, -bound), bound)
        t_high, t_low = terms(coef)
        gt_high, gt_low = terms(g_t)
        u = dot(
            jnp.concatenate([t_high, t_low, t_high], axis=1),
            jnp.concatenate([gt_high, gt_high, gt_low], axis=0),
        )
        part_high, part_low = terms(u)
        u_high[level] = part_high.reshape(channels, half, wide)
        u_low[level] = part_low.reshape(channels, half, wide)

    for c in range(channels):
        highs = [u_high[level, c] for level in range(LEVELS)]
        lows = [u_low[level, c] for level in range(LEVELS)]
        back = dot(at_cat, jnp.concatenate(highs + lows + highs, axis=0))
        above_out[c] = back[:BORDER, :cols]
        own_out[c] = back[BORDER:, :cols]
        corner_out[c] = pack_rows(back[:BORDER, cols:], 0)
        left_out[c] = pack_rows(back[BORDER:, cols:], 0)


def last_kernel(
    radius, start_ref, dirty_ref, sampling_ref, basis_ref, energy_ref, own_ref, below_ref, right_ref, corner_ref,
    image_ref, dual_ref,
):
    channels, rows, cols = start_ref.shape
    rank = basis_ref.shape[0]
    groups = rows // 8
    energy = jnp.sum(jnp.sum(energy_ref[...], axis=0, keepdims=True), axis=1, keepdims=True)
    factor = jnp.maximum(0.0, 1.0 - DUAL_STEP * radius / jnp.sqrt(energy + NORM_EPS))
    factor = jnp.broadcast_to(factor, (rows, cols))
    edge = lane_iota((rows, cols)) >= cols - BORDER
    weights = [jnp.zeros((rows, cols), jnp.float32) for r in range(rank)]
    for c in range(channels):
        field = start_ref[c]
        gain = sampling_ref[c]
        dual = factor * (DUAL_STEP * gain * field - DUAL_STEP * dirty_ref[c])
        dual_ref[c] = dual
        strip = unpack_rows(right_ref[c] + corner_ref[c], cols - BORDER, groups)
        prior = own_ref[c] + below_ref[c] + jnp.where(edge, strip, 0.0)
        stepped = field - PRIMAL_STEP * (gain * dual + (WEIGHT * BAND_STEP) * prior)
        for r in range(rank):
            weights[r] = weights[r] + basis_ref[r, c : c + 1, :] * stepped
    for c in range(channels):
        total = basis_ref[0, c : c + 1, :] * weights[0]
        for r in range(1, rank):
            total = total + basis_ref[r, c : c + 1, :] * weights[r]
        image_ref[c] = jnp.maximum(total, 0.0)


def shift(axis_sizes, steps):
    pairs = []
    for a in range(axis_sizes[0]):
        for b in range(axis_sizes[1]):
            to_a, to_b = a + steps[0], b + steps[1]
            if 0 <= to_a < axis_sizes[0] and 0 <= to_b < axis_sizes[1]:
                pairs.append((a * axis_sizes[1] + b, to_a * axis_sizes[1] + to_b))
    return pairs


def whole_sum(value):
    for axis in ("fy", "fx"):
        count = lax.axis_size(axis)
        if count & (count - 1):
            value = lax.psum(value, axis)
        else:
            step = 1
            while step < count:
                value = value + lax.ppermute(value, axis, [(i, i ^ step) for i in range(count)])
                step *= 2
    return value


def per_device(start_image, dirty, sampling, basis_seed, margin):
    channels, rows, cols = start_image.shape
    sizes = (lax.axis_size("fy"), lax.axis_size("fx"))
    half = 2 * rows
    wide = cols + LANES
    radius = BALL_SCALE * math.sqrt(channels * rows * cols * sizes[0] * sizes[1])
    f32 = jnp.float32
    image_shape = jax.ShapeDtypeStruct((channels, rows, cols), f32)
    pack_shape = jax.ShapeDtypeStruct((channels, 8, LANES), f32)
    params = pltpu.CompilerParams(vmem_limit_bytes=48 * 1024 * 1024)

    def moved(value, steps):
        return lax.ppermute(value, ("fy", "fx"), shift(sizes, steps))

    above = moved(start_image, (1, 0))
    energy, pack = pl.pallas_call(
        first_kernel,
        out_shape=(jax.ShapeDtypeStruct((8, cols), f32), pack_shape),
        compiler_params=params,
        name="first",
    )(start_image, dirty, sampling)
    left = moved(pack, (0, 1))
    corner = moved(pack, (1, 1))
    basis = pl.pallas_call(
        basis_kernel,
        out_shape=jax.ShapeDtypeStruct((basis_seed.shape[1], channels, LANES), f32),
        compiler_params=params,
        name="basis",
    )(basis_seed)
    energy = whole_sum(energy)

    table = row_table(rows)
    table_t = np.ascontiguousarray(table.reshape(LEVELS, half, rows + BORDER).transpose(0, 2, 1))
    col = col_table(cols)
    col_t = np.ascontiguousarray(col.transpose(0, 2, 1))
    vmem = pl.BlockSpec(memory_space=pltpu.VMEM)
    own_part, above_part, left_part, corner_part = pl.pallas_call(
        bank_kernel,
        out_shape=(image_shape, image_shape, pack_shape, pack_shape),
        in_specs=[pl.BlockSpec(memory_space=pltpu.SMEM)] + [vmem] * 8,
        scratch_shapes=[
            pltpu.VMEM((LEVELS, channels, half, wide), jnp.bfloat16) for i in range(4)
        ],
        compiler_params=params,
        name="bank",
    )(margin.reshape(-1), start_image, above, left, corner, table, table_t, col, col_t)
    below = moved(above_part, (-1, 0))
    right = moved(left_part, (0, -1))
    corner_back = moved(corner_part, (-1, -1))

    def last(*refs):
        last_kernel(radius, *refs)

    return pl.pallas_call(
        last,
        out_shape=(image_shape, image_shape),
        compiler_params=params,
        name="last",
    )(start_image, dirty, sampling, basis, energy, own_part, below, right, corner_back)


def solution(mesh):
    return jax.shard_map(
        per_device,
        mesh=mesh,
        in_specs=(
            P(None, "fy", "fx"),
            P(None, "fy", "fx"),
            P(None, "fy", "fx"),
            P(),
            P("fy", "fx", None, None),
        ),
        out_specs=(P(None, "fy", "fx"), P(None, "fy", "fx")),
        check_vma=False,
    )
```

```python
import math

import jax
import jax.numpy as jnp
import numpy as np
from jax import lax
from jax.experimental import pallas as pl
from jax.experimental.pallas import tpu as pltpu
from jax.sharding import PartitionSpec as P

LEVELS = 2
BORDER = 32
LANES = 128


DAUBECHIES = [
    -0.00011747678400228192,
    0.0006754494059985568,
    -0.0003917403729959771,
    -0.00487035299301066,
    0.008746094047015655,
    0.013981027917015516,
    -0.04408825393106472,
    -0.01736930100202211,
    0.128747426620186,
    0.00047248457399797254,
    -0.2840155429624281,
    -0.015829105256023893,
    0.5853546836548691,
    0.6756307362980128,
    0.3128715909144659,
    0.05441584224308161,
]
DUAL_STEP = 0.5
PRIMAL_STEP = 0.5
CLIP_LEVEL = 0.08
BALL_SCALE = 0.8
NORM_EPS = 1e-06
WEIGHT = 1.0 / math.sqrt(LEVELS)
BAND_STEP = DUAL_STEP * WEIGHT

LOW = [tap / math.sqrt(2.0) for tap in DAUBECHIES]
HIGH = [(-1.0) ** k * LOW[len(LOW) - 1 - k] for k in range(len(LOW))]


def band(taps, extent, dilation):
    matrix = np.zeros((BORDER + extent, extent), np.float32)
    for k, tap in enumerate(taps):
        for i in range(extent):
            matrix[i - k * dilation + BORDER, i] += np.float32(tap)
    return matrix


def row_table(rows):
    return np.concatenate(
        [band(taps, rows, 2**level).T for level in range(LEVELS) for taps in (LOW, HIGH)], axis=0
    )


def col_table(cols):
    table = np.zeros((LEVELS, cols + LANES, 2 * cols), np.float32)
    for level in range(LEVELS):
        for half, taps in enumerate((LOW, HIGH)):
            matrix = band(taps, cols, 2**level)
            table[level, :cols, half * cols : (half + 1) * cols] = matrix[BORDER:]
            table[level, cols : cols + BORDER, half * cols : (half + 1) * cols] = matrix[:BORDER]
    return table


def terms(value):
    high = value.astype(jnp.bfloat16)
    low = (value - high.astype(jnp.float32)).astype(jnp.bfloat16)
    return high, low


def dot(a, b):
    return lax.dot_general(a, b, (((1,), (0,)), ((), ())), preferred_element_type=jnp.float32)


def lane_iota(shape):
    return lax.broadcasted_iota(jnp.int32, shape, len(shape) - 1)


def row_iota(shape):
    return lax.broadcasted_iota(jnp.int32, shape, len(shape) - 2)


def pack_rows(strip, offset):
    groups = strip.shape[0] // 8
    lane = lane_iota((8, LANES))
    packed = None
    for q in range(groups):
        piece = strip[8 * q : 8 * q + 8]
        shift = (BORDER * q - offset) % LANES
        if shift:
            piece = pltpu.roll(piece, shift, 1)
        packed = piece if packed is None else jnp.where(lane >= BORDER * q, piece, packed)
    return packed


def unpack_rows(packed, offset, groups):
    pieces = []
    for q in range(groups):
        shift = (offset - BORDER * q) % LANES
        pieces.append(pltpu.roll(packed, shift, 1) if shift else packed)
    return jnp.concatenate(pieces, axis=0)


def first_kernel(
    start_hbm, dirty_hbm, sampling_hbm, energy_ref, pack_ref, own_ref, gain_ref, shifted_ref, dirty_ref, sems
):
    channels, rows, cols = own_ref.shape
    parts = sems.shape[0]
    size = channels // parts
    copies = []
    for part in range(parts):
        at = pl.ds(part * size, size)
        trio = [
            pltpu.make_async_copy(source.at[at], target.at[at], sems.at[part, k])
            for k, (source, target) in enumerate(
                ((start_hbm, own_ref), (sampling_hbm, gain_ref), (dirty_hbm, dirty_ref))
            )
        ]
        for copy in trio:
            copy.start()
        copies.append(trio)
    total = jnp.zeros((8, cols), jnp.float32)
    for part in range(parts):
        for copy in copies[part]:
            copy.wait()
        for c in range(part * size, (part + 1) * size):
            field = own_ref[c]
            shifted = DUAL_STEP * gain_ref[c] * field - DUAL_STEP * dirty_ref[c]
            shifted_ref[c] = shifted
            square = shifted * shifted
            for q in range(rows // 8):
                total = total + square[8 * q : 8 * q + 8]
            pack_ref[c] = pack_rows(field, cols - BORDER)
    energy_ref[...] = total


def prepare_kernel(
    margin_ref, seed_ref, after_ref, rows_hbm, rows_t_hbm, cols_hbm,
    basis_ref, a_ref, at_ref, g_ref, rows_ref, rows_t_ref, cols_ref, sems,
):
    copies = [
        pltpu.make_async_copy(rows_hbm, rows_ref, sems.at[0]),
        pltpu.make_async_copy(rows_t_hbm, rows_t_ref, sems.at[1]),
    ]
    for level in range(LEVELS):
        for k in range(2):
            span = pl.ds(k * (cols_ref.shape[1] // 2), cols_ref.shape[1] // 2)
            copies.append(
                pltpu.make_async_copy(
                    cols_hbm.at[level, span], cols_ref.at[level, span], sems.at[2 + 2 * level + k]
                )
            )
    for copy in copies:
        copy.start()

    rank, channels = seed_ref.shape
    eye = row_iota((channels, channels)) == lane_iota((channels, channels))
    columns = []
    for r in range(rank):
        row = jnp.broadcast_to(seed_ref[r : r + 1, :], (channels, channels))
        column = jnp.sum(jnp.where(eye, row, 0.0), axis=1, keepdims=True)
        columns.append(jnp.broadcast_to(column, (channels, LANES)))
    for r in range(rank):
        vector = columns[r]
        vector = vector / jnp.sqrt(jnp.sum(vector * vector, axis=0, keepdims=True))
        basis_ref[r] = vector
        for later in range(r + 1, rank):
            along = jnp.sum(vector * columns[later], axis=0, keepdims=True)
            columns[later] = columns[later] - along * vector

    for copy in copies:
        copy.wait()
    half, tall = rows_ref.shape[0] // LEVELS, rows_ref.shape[1]
    wide, double = cols_ref.shape[1:]
    cols = double // 2
    first_row = lax.axis_index("fy") == 0
    first_col = lax.axis_index("fx") == 0
    position = lane_iota((half, tall)) - BORDER
    position_t = row_iota((tall, half)) - BORDER
    a_parts, at_parts = [], []
    for level in range(LEVELS):
        width = jnp.where(first_row, 0, margin_ref[0, 0, level, 0])
        a_parts.append(jnp.where(position >= -width, rows_ref[level * half : (level + 1) * half], 0.0))
        at_parts.append(jnp.where(position_t >= -width, rows_t_ref[level], 0.0))
    a_high, a_low = terms(jnp.concatenate(a_parts, axis=0))
    a_ref[...] = jnp.concatenate([a_high, a_high, a_low], axis=1)
    at_pairs = [terms(part) for part in at_parts]
    at_ref[...] = jnp.concatenate(
        [pair[0] for pair in at_pairs] * 2 + [pair[1] for pair in at_pairs], axis=1
    )
    at = row_iota((wide, double))
    for level in range(LEVELS):
        width = jnp.where(first_col, 0, margin_ref[0, 0, level, 1])
        g = jnp.where((at < cols) | (at >= cols + BORDER - width), cols_ref[level], 0.0)
        g_high, g_low = terms(g)
        g_ref[level, 0] = g_high
        g_ref[level, 1] = g_low


def dot_t(a, b):
    return lax.dot_general(a, b, (((1,), (1,)), ((), ())), preferred_element_type=jnp.float32)


def bank_kernel(
    own_ref, above_ref, left_ref, corner_ref, a_ref, at_ref, g_ref,
    own_out, above_out, left_out, corner_out, z_high, z_low, u_high, u_low,
):
    channels, rows, cols = own_ref.shape
    groups = rows // 8
    wide = cols + LANES
    half = 2 * rows

    for c in range(channels):
        upper = jnp.concatenate([above_ref[c], unpack_rows(corner_ref[c], 0, groups)], axis=1)
        lower = jnp.concatenate([own_ref[c], unpack_rows(left_ref[c], 0, groups)], axis=1)
        e_high, e_low = terms(jnp.concatenate([upper, lower], axis=0))
        z = dot(a_ref[...], jnp.concatenate([e_high, e_low, e_high], axis=0))
        part_high, part_low = terms(z)
        for level in range(LEVELS):
            z_high[level, c] = part_high[level * half : (level + 1) * half]
            z_low[level, c] = part_low[level * half : (level + 1) * half]

    low_rows = row_iota((half, 2 * cols)) < rows
    low_cols = lane_iota((half, 2 * cols)) < cols
    bound = jnp.where(low_rows & low_cols, 0.0, CLIP_LEVEL / BAND_STEP)
    bound = jnp.broadcast_to(bound[None], (channels, half, 2 * cols)).reshape(channels * half, 2 * cols)
    for level in range(LEVELS):
        zh = z_high[level].reshape(channels * half, wide)
        zl = z_low[level].reshape(channels * half, wide)
        g_high, g_low = g_ref[level, 0], g_ref[level, 1]
        coef = dot(jnp.concatenate([zh, zl, zh], axis=1), jnp.concatenate([g_high, g_high, g_low], axis=0))
        coef = jnp.minimum(jnp.maximum(coef, -bound), bound)
        t_high, t_low = terms(coef)
        u = dot_t(
            jnp.concatenate([t_high, t_low, t_high], axis=1),
            jnp.concatenate([g_high, g_high, g_low], axis=1),
        )
        part_high, part_low = terms(u)
        u_high[level] = part_high.reshape(channels, half, wide)
        u_low[level] = part_low.reshape(channels, half, wide)

    for c in range(channels):
        highs = [u_high[level, c] for level in range(LEVELS)]
        lows = [u_low[level, c] for level in range(LEVELS)]
        back = dot(at_ref[...], jnp.concatenate(highs + lows + highs, axis=0))
        above_out[c] = back[:BORDER, :cols]
        own_out[c] = back[BORDER:, :cols]
        corner_out[c] = pack_rows(back[:BORDER, cols:], 0)
        left_out[c] = pack_rows(back[BORDER:, cols:], 0)


def last_kernel(
    radius, start_ref, shifted_ref, sampling_ref, basis_ref, energy_ref, own_ref, below_ref, right_ref, corner_ref,
    image_ref, dual_ref,
):
    channels, rows, cols = start_ref.shape
    rank = basis_ref.shape[0]
    groups = rows // 8
    energy = jnp.sum(jnp.sum(energy_ref[...], axis=0, keepdims=True), axis=1, keepdims=True)
    factor = jnp.maximum(0.0, 1.0 - DUAL_STEP * radius / jnp.sqrt(energy + NORM_EPS))
    factor = jnp.broadcast_to(factor, (rows, cols))
    edge = lane_iota((rows, cols)) >= cols - BORDER
    weights = [jnp.zeros((rows, cols), jnp.float32) for r in range(rank)]
    for c in range(channels):
        field = start_ref[c]
        gain = sampling_ref[c]
        dual = factor * shifted_ref[c]
        dual_ref[c] = dual
        strip = unpack_rows(right_ref[c] + corner_ref[c], cols - BORDER, groups)
        prior = own_ref[c] + below_ref[c] + jnp.where(edge, strip, 0.0)
        stepped = field - PRIMAL_STEP * (gain * dual + (WEIGHT * BAND_STEP) * prior)
        for r in range(rank):
            weights[r] = weights[r] + basis_ref[r, c : c + 1, :] * stepped
    for c in range(channels):
        total = basis_ref[0, c : c + 1, :] * weights[0]
        for r in range(1, rank):
            total = total + basis_ref[r, c : c + 1, :] * weights[r]
        image_ref[c] = jnp.maximum(total, 0.0)


def shift(axis_sizes, steps):
    return [
        (
            a * axis_sizes[1] + b,
            (a + steps[0]) % axis_sizes[0] * axis_sizes[1] + (b + steps[1]) % axis_sizes[1],
        )
        for a in range(axis_sizes[0])
        for b in range(axis_sizes[1])
    ]


def whole_sum(value):
    for axis in ("fy", "fx"):
        count = lax.axis_size(axis)
        if count & (count - 1):
            value = lax.psum(value, axis)
        else:
            step = 1
            while step < count:
                value = value + lax.ppermute(value, axis, [(i, i ^ step) for i in range(count)])
                step *= 2
    return value


def per_device(start_image, dirty, sampling, basis_seed, margin):
    channels, rows, cols = start_image.shape
    rank = basis_seed.shape[1]
    sizes = (lax.axis_size("fy"), lax.axis_size("fx"))
    half = 2 * rows
    tall = rows + BORDER
    wide = cols + LANES
    radius = BALL_SCALE * math.sqrt(channels * rows * cols * sizes[0] * sizes[1])
    f32, bf16 = jnp.float32, jnp.bfloat16
    image_shape = jax.ShapeDtypeStruct((channels, rows, cols), f32)
    pack_shape = jax.ShapeDtypeStruct((channels, 8, LANES), f32)
    params = pltpu.CompilerParams(vmem_limit_bytes=48 * 1024 * 1024)
    vmem = pl.BlockSpec(memory_space=pltpu.VMEM)
    smem = pl.BlockSpec(memory_space=pltpu.SMEM)
    hbm = pl.BlockSpec(memory_space=pltpu.HBM)
    anywhere = pl.BlockSpec(memory_space=pl.ANY)

    def kept(value):
        return pltpu.with_memory_space_constraint(value, pltpu.HBM)

    def moved(value, steps):
        return lax.ppermute(value, ("fy", "fx"), shift(sizes, steps))

    above = moved(start_image, (1, 0))
    energy, pack, own, gain, shifted = pl.pallas_call(
        first_kernel,
        out_shape=(jax.ShapeDtypeStruct((8, cols), f32), pack_shape, image_shape, image_shape, image_shape),
        in_specs=[hbm] * 3,
        out_specs=(vmem,) * 5,
        scratch_shapes=[pltpu.VMEM((channels, rows, cols), f32), pltpu.SemaphoreType.DMA((4, 3))],
        compiler_params=params,
        name="first",
    )(kept(start_image), kept(dirty), kept(sampling))
    left = moved(pack, (0, 1))
    corner = moved(pack, (1, 1))

    table = row_table(rows)
    table_t = np.ascontiguousarray(table.reshape(LEVELS, half, tall).transpose(0, 2, 1))
    basis, a, a_t, g = pl.pallas_call(
        prepare_kernel,
        out_shape=(
            jax.ShapeDtypeStruct((rank, channels, LANES), f32),
            jax.ShapeDtypeStruct((LEVELS * half, 3 * tall), bf16),
            jax.ShapeDtypeStruct((tall, 3 * LEVELS * half), bf16),
            jax.ShapeDtypeStruct((LEVELS, 2, wide, 2 * cols), bf16),
        ),
        in_specs=[smem, vmem, anywhere, hbm, hbm, hbm],
        out_specs=(vmem,) * 4,
        scratch_shapes=[
            pltpu.VMEM((LEVELS * half, tall), f32),
            pltpu.VMEM((LEVELS, tall, half), f32),
            pltpu.VMEM((LEVELS, wide, 2 * cols), f32),
            pltpu.SemaphoreType.DMA((2 + 2 * LEVELS,)),
        ],
        compiler_params=params,
        name="prepare",
    )(margin, basis_seed.T, pack, kept(jnp.asarray(table)), kept(jnp.asarray(table_t)), kept(jnp.asarray(col_table(cols))))
    energy = whole_sum(energy)

    own_part, above_part, left_part, corner_part = pl.pallas_call(
        bank_kernel,
        out_shape=(image_shape, image_shape, pack_shape, pack_shape),
        in_specs=[vmem] * 7,
        out_specs=(vmem,) * 4,
        scratch_shapes=[pltpu.VMEM((LEVELS, channels, half, wide), bf16) for i in range(4)],
        compiler_params=params,
        name="bank",
    )(own, above, left, corner, a, a_t, g)
    below = moved(above_part, (-1, 0))
    right = moved(left_part, (0, -1))
    corner_back = moved(corner_part, (-1, -1))

    def last(*refs):
        last_kernel(radius, *refs)

    return pl.pallas_call(
        last,
        out_shape=(image_shape, image_shape),
        in_specs=[vmem] * 9,
        compiler_params=params,
        name="last",
    )(own, shifted, gain, basis, energy, own_part, below, right, corner_back)


def solution(mesh):
    return jax.shard_map(
        per_device,
        mesh=mesh,
        in_specs=(
            P(None, "fy", "fx"),
            P(None, "fy", "fx"),
            P(None, "fy", "fx"),
            P(),
            P("fy", "fx", None, None),
        ),
        out_specs=(P(None, "fy", "fx"), P(None, "fy", "fx")),
        check_vma=False,
    )
```

```python
import math

import jax
import jax.numpy as jnp
import numpy as np
from jax import lax
from jax.experimental import pallas as pl
from jax.experimental.pallas import tpu as pltpu
from jax.sharding import PartitionSpec as P

LEVELS = 2
BORDER = 32
LANES = 128


DAUBECHIES = [
    -0.00011747678400228192,
    0.0006754494059985568,
    -0.0003917403729959771,
    -0.00487035299301066,
    0.008746094047015655,
    0.013981027917015516,
    -0.04408825393106472,
    -0.01736930100202211,
    0.128747426620186,
    0.00047248457399797254,
    -0.2840155429624281,
    -0.015829105256023893,
    0.5853546836548691,
    0.6756307362980128,
    0.3128715909144659,
    0.05441584224308161,
]
DUAL_STEP = 0.5
PRIMAL_STEP = 0.5
CLIP_LEVEL = 0.08
BALL_SCALE = 0.8
NORM_EPS = 1e-06
WEIGHT = 1.0 / math.sqrt(LEVELS)
BAND_STEP = DUAL_STEP * WEIGHT

LOW = [tap / math.sqrt(2.0) for tap in DAUBECHIES]
HIGH = [(-1.0) ** k * LOW[len(LOW) - 1 - k] for k in range(len(LOW))]


def band(taps, extent, dilation):
    matrix = np.zeros((BORDER + extent, extent), np.float32)
    for k, tap in enumerate(taps):
        for i in range(extent):
            matrix[i - k * dilation + BORDER, i] += np.float32(tap)
    return matrix


def row_table(rows):
    return np.concatenate(
        [band(taps, rows, 2**level).T for level in range(LEVELS) for taps in (LOW, HIGH)], axis=0
    )


def col_table(cols):
    table = np.zeros((LEVELS, cols + LANES, 2 * cols), np.float32)
    for level in range(LEVELS):
        for half, taps in enumerate((LOW, HIGH)):
            matrix = band(taps, cols, 2**level)
            table[level, :cols, half * cols : (half + 1) * cols] = matrix[BORDER:]
            table[level, cols : cols + BORDER, half * cols : (half + 1) * cols] = matrix[:BORDER]
    return table


def terms(value):
    high = value.astype(jnp.bfloat16)
    low = (value - high.astype(jnp.float32)).astype(jnp.bfloat16)
    return high, low


def dot(a, b):
    return lax.dot_general(a, b, (((1,), (0,)), ((), ())), preferred_element_type=jnp.float32)


def lane_iota(shape):
    return lax.broadcasted_iota(jnp.int32, shape, len(shape) - 1)


def row_iota(shape):
    return lax.broadcasted_iota(jnp.int32, shape, len(shape) - 2)


def pack_rows(strip, offset):
    groups = strip.shape[0] // 8
    lane = lane_iota((8, LANES))
    packed = None
    for q in range(groups):
        piece = strip[8 * q : 8 * q + 8]
        shift = (BORDER * q - offset) % LANES
        if shift:
            piece = pltpu.roll(piece, shift, 1)
        packed = piece if packed is None else jnp.where(lane >= BORDER * q, piece, packed)
    return packed


def unpack_rows(packed, offset, groups):
    pieces = []
    for q in range(groups):
        shift = (offset - BORDER * q) % LANES
        pieces.append(pltpu.roll(packed, shift, 1) if shift else packed)
    return jnp.concatenate(pieces, axis=0)


def first_kernel(
    start_hbm, dirty_hbm, sampling_hbm, energy_ref, pack_ref, own_ref, gain_ref, shifted_ref, dirty_ref, sems
):
    channels, rows, cols = own_ref.shape
    parts = sems.shape[0]
    size = channels // parts
    copies = []
    for part in range(parts):
        at = pl.ds(part * size, size)
        trio = [
            pltpu.make_async_copy(source.at[at], target.at[at], sems.at[part, k])
            for k, (source, target) in enumerate(
                ((start_hbm, own_ref), (sampling_hbm, gain_ref), (dirty_hbm, dirty_ref))
            )
        ]
        for copy in trio:
            copy.start()
        copies.append(trio)
    total = jnp.zeros((8, cols), jnp.float32)
    for part in range(parts):
        for copy in copies[part]:
            copy.wait()
        for c in range(part * size, (part + 1) * size):
            field = own_ref[c]
            shifted = DUAL_STEP * gain_ref[c] * field - DUAL_STEP * dirty_ref[c]
            shifted_ref[c] = shifted
            square = shifted * shifted
            for q in range(rows // 8):
                total = total + square[8 * q : 8 * q + 8]
            pack_ref[c] = pack_rows(field, cols - BORDER)
    energy_ref[...] = total


def prepare_kernel(
    margin_ref, seed_ref, after_ref, rows_hbm, rows_t_hbm, cols_hbm,
    basis_ref, a_ref, at_ref, g_ref, rows_ref, rows_t_ref, cols_ref, sems,
):
    copies = [
        pltpu.make_async_copy(rows_hbm, rows_ref, sems.at[0]),
        pltpu.make_async_copy(rows_t_hbm, rows_t_ref, sems.at[1]),
    ]
    for level in range(LEVELS):
        for k in range(2):
            span = pl.ds(k * (cols_ref.shape[1] // 2), cols_ref.shape[1] // 2)
            copies.append(
                pltpu.make_async_copy(
                    cols_hbm.at[level, span], cols_ref.at[level, span], sems.at[2 + 2 * level + k]
                )
            )
    for copy in copies:
        copy.start()

    rank, channels = seed_ref.shape
    eye = row_iota((channels, channels)) == lane_iota((channels, channels))
    columns = []
    for r in range(rank):
        row = jnp.broadcast_to(seed_ref[r : r + 1, :], (channels, channels))
        column = jnp.sum(jnp.where(eye, row, 0.0), axis=1, keepdims=True)
        columns.append(jnp.broadcast_to(column, (channels, LANES)))
    for r in range(rank):
        vector = columns[r]
        vector = vector / jnp.sqrt(jnp.sum(vector * vector, axis=0, keepdims=True))
        basis_ref[r] = vector
        for later in range(r + 1, rank):
            along = jnp.sum(vector * columns[later], axis=0, keepdims=True)
            columns[later] = columns[later] - along * vector

    for copy in copies:
        copy.wait()
    half, tall = rows_ref.shape[0] // LEVELS, rows_ref.shape[1]
    wide, double = cols_ref.shape[1:]
    cols = double // 2
    first_row = lax.axis_index("fy") == 0
    first_col = lax.axis_index("fx") == 0
    position = lane_iota((half, tall)) - BORDER
    position_t = row_iota((tall, half)) - BORDER
    a_parts, at_parts = [], []
    for level in range(LEVELS):
        width = jnp.where(first_row, 0, margin_ref[0, 0, level, 0])
        a_parts.append(jnp.where(position >= -width, rows_ref[level * half : (level + 1) * half], 0.0))
        at_parts.append(jnp.where(position_t >= -width, rows_t_ref[level], 0.0))
    a_high, a_low = terms(jnp.concatenate(a_parts, axis=0))
    a_ref[...] = jnp.concatenate([a_high, a_high, a_low], axis=1)
    at_pairs = [terms(part) for part in at_parts]
    at_ref[...] = jnp.concatenate(
        [pair[0] for pair in at_pairs] * 2 + [pair[1] for pair in at_pairs], axis=1
    )
    at = row_iota((wide, double))
    for level in range(LEVELS):
        width = jnp.where(first_col, 0, margin_ref[0, 0, level, 1])
        g = jnp.where((at < cols) | (at >= cols + BORDER - width), cols_ref[level], 0.0)
        g_high, g_low = terms(g)
        g_ref[level, 0] = g_high
        g_ref[level, 1] = g_low


def dot_t(a, b):
    return lax.dot_general(a, b, (((1,), (1,)), ((), ())), preferred_element_type=jnp.float32)


def bank_kernel(
    own_ref, above_ref, left_ref, corner_ref, a_ref, at_ref, g_ref, after_ref,
    own_out, above_out, left_out, corner_out, z_high, z_low, u_high, u_low,
):
    channels, rows, cols = own_ref.shape
    groups = rows // 8
    wide = cols + LANES
    half = 2 * rows

    for c in range(channels):
        upper = jnp.concatenate([above_ref[c], unpack_rows(corner_ref[c], 0, groups)], axis=1)
        lower = jnp.concatenate([own_ref[c], unpack_rows(left_ref[c], 0, groups)], axis=1)
        e_high, e_low = terms(jnp.concatenate([upper, lower], axis=0))
        z = dot(a_ref[...], jnp.concatenate([e_high, e_low, e_high], axis=0))
        part_high, part_low = terms(z)
        for level in range(LEVELS):
            z_high[level, c] = part_high[level * half : (level + 1) * half]
            z_low[level, c] = part_low[level * half : (level + 1) * half]

    low_rows = row_iota((half, 2 * cols)) < rows
    low_cols = lane_iota((half, 2 * cols)) < cols
    bound = jnp.where(low_rows & low_cols, 0.0, CLIP_LEVEL / BAND_STEP)
    bound = jnp.broadcast_to(bound[None], (channels, half, 2 * cols)).reshape(channels * half, 2 * cols)
    for level in range(LEVELS):
        zh = z_high[level].reshape(channels * half, wide)
        zl = z_low[level].reshape(channels * half, wide)
        g_high, g_low = g_ref[level, 0], g_ref[level, 1]
        coef = dot(jnp.concatenate([zh, zl, zh], axis=1), jnp.concatenate([g_high, g_high, g_low], axis=0))
        coef = jnp.minimum(jnp.maximum(coef, -bound), bound)
        t_high, t_low = terms(coef)
        u = dot_t(
            jnp.concatenate([t_high, t_low, t_high], axis=1),
            jnp.concatenate([g_high, g_high, g_low], axis=1),
        )
        part_high, part_low = terms(u)
        u_high[level] = part_high.reshape(channels, half, wide)
        u_low[level] = part_low.reshape(channels, half, wide)

    for c in range(channels):
        highs = [u_high[level, c] for level in range(LEVELS)]
        lows = [u_low[level, c] for level in range(LEVELS)]
        back = dot(at_ref[...], jnp.concatenate(highs + lows + highs, axis=0))
        above_out[BORDER * c : BORDER * (c + 1)] = back[:BORDER, :cols]
        own_out[c] = back[BORDER:, :cols]
        corner_out[8 * c : 8 * (c + 1)] = pack_rows(back[:BORDER, cols:], 0)
        left_out[8 * c : 8 * (c + 1)] = pack_rows(back[BORDER:, cols:], 0)


def last_kernel(
    radius, start_ref, shifted_ref, sampling_ref, basis_ref, energy_ref, own_ref, below_ref, right_ref, corner_ref,
    image_ref, dual_ref,
):
    channels, rows, cols = start_ref.shape
    rank = basis_ref.shape[0]
    groups = rows // 8
    energy = energy_ref[...]
    for ref in (below_ref, right_ref, corner_ref):
        energy = energy + ref[pl.ds(ref.shape[0] - 8, 8)]
    energy = jnp.sum(jnp.sum(energy, axis=0, keepdims=True), axis=1, keepdims=True)
    factor = jnp.maximum(0.0, 1.0 - DUAL_STEP * radius / jnp.sqrt(energy + NORM_EPS))
    factor = jnp.broadcast_to(factor, (rows, cols))
    edge = lane_iota((rows, cols)) >= cols - BORDER
    weights = [jnp.zeros((rows, cols), jnp.float32) for r in range(rank)]
    for c in range(channels):
        field = start_ref[c]
        gain = sampling_ref[c]
        dual = factor * shifted_ref[c]
        dual_ref[c] = dual
        strip = right_ref[8 * c : 8 * (c + 1)] + corner_ref[8 * c : 8 * (c + 1)]
        strip = unpack_rows(strip, cols - BORDER, groups)
        prior = own_ref[c] + below_ref[BORDER * c : BORDER * (c + 1)] + jnp.where(edge, strip, 0.0)
        stepped = field - PRIMAL_STEP * (gain * dual + (WEIGHT * BAND_STEP) * prior)
        for r in range(rank):
            weights[r] = weights[r] + basis_ref[r, c : c + 1, :] * stepped
    for c in range(channels):
        total = basis_ref[0, c : c + 1, :] * weights[0]
        for r in range(1, rank):
            total = total + basis_ref[r, c : c + 1, :] * weights[r]
        image_ref[c] = jnp.maximum(total, 0.0)


def shift(axis_sizes, steps):
    return [
        (
            a * axis_sizes[1] + b,
            (a + steps[0]) % axis_sizes[0] * axis_sizes[1] + (b + steps[1]) % axis_sizes[1],
        )
        for a in range(axis_sizes[0])
        for b in range(axis_sizes[1])
    ]


def add_kernel(value_ref, arrived_ref, *refs):
    refs[-1][...] = value_ref[...] + arrived_ref[...]


def doubling():
    rounds = []
    for axis in ("fx", "fy"):
        step = 2
        while step < lax.axis_size(axis):
            rounds.append((axis, step))
            step *= 2
    return rounds


def partner(value, round_):
    axis, step = round_
    return lax.ppermute(value, axis, [(i, i ^ step) for i in range(lax.axis_size(axis))])


def stamp_kernel(value_ref, arrived_ref, above_in, left_in, corner_in, total_ref, above_ref, left_ref, corner_ref):
    total = value_ref[...] + arrived_ref[...]
    total_ref[...] = total
    for ref in (above_ref, left_ref, corner_ref):
        ref[pl.ds(ref.shape[0] - 8, 8)] = total


def added(value, arrived, *after):
    return pl.pallas_call(
        add_kernel,
        out_shape=jax.ShapeDtypeStruct(value.shape, value.dtype),
        in_specs=[pl.BlockSpec(memory_space=pltpu.VMEM)] * 2 + [pl.BlockSpec(memory_space=pl.ANY)] * len(after),
        out_specs=pl.BlockSpec(memory_space=pltpu.VMEM),
        compiler_params=pltpu.CompilerParams(vmem_limit_bytes=1024 * 1024),
        name="add",
    )(value, arrived, *after)


def per_device(start_image, dirty, sampling, basis_seed, margin):
    channels, rows, cols = start_image.shape
    rank = basis_seed.shape[1]
    sizes = (lax.axis_size("fy"), lax.axis_size("fx"))
    half = 2 * rows
    tall = rows + BORDER
    wide = cols + LANES
    radius = BALL_SCALE * math.sqrt(channels * rows * cols * sizes[0] * sizes[1])
    f32, bf16 = jnp.float32, jnp.bfloat16
    image_shape = jax.ShapeDtypeStruct((channels, rows, cols), f32)
    pack_shape = jax.ShapeDtypeStruct((channels, 8, LANES), f32)
    params = pltpu.CompilerParams(vmem_limit_bytes=24 * 1024 * 1024)
    vmem = pl.BlockSpec(memory_space=pltpu.VMEM)
    smem = pl.BlockSpec(memory_space=pltpu.SMEM)
    hbm = pl.BlockSpec(memory_space=pltpu.HBM)
    anywhere = pl.BlockSpec(memory_space=pl.ANY)

    def kept(value):
        return pltpu.with_memory_space_constraint(value, pltpu.HBM)

    def moved(value, steps):
        return lax.ppermute(value, ("fy", "fx"), shift(sizes, steps))

    above = moved(start_image, (1, 0))
    energy, pack, own, gain, shifted = pl.pallas_call(
        first_kernel,
        out_shape=(jax.ShapeDtypeStruct((8, cols), f32), pack_shape, image_shape, image_shape, image_shape),
        in_specs=[hbm] * 3,
        out_specs=(vmem,) * 5,
        scratch_shapes=[pltpu.VMEM((channels, rows, cols), f32), pltpu.SemaphoreType.DMA((4, 3))],
        compiler_params=params,
        name="first",
    )(kept(start_image), kept(dirty), kept(sampling))
    left = moved(pack, (0, 1))
    corner = moved(pack, (1, 1))

    table = row_table(rows)
    table_t = np.ascontiguousarray(table.reshape(LEVELS, half, tall).transpose(0, 2, 1))
    basis, a, a_t, g = pl.pallas_call(
        prepare_kernel,
        out_shape=(
            jax.ShapeDtypeStruct((rank, channels, LANES), f32),
            jax.ShapeDtypeStruct((LEVELS * half, 3 * tall), bf16),
            jax.ShapeDtypeStruct((tall, 3 * LEVELS * half), bf16),
            jax.ShapeDtypeStruct((LEVELS, 2, wide, 2 * cols), bf16),
        ),
        in_specs=[smem, vmem, anywhere, hbm, hbm, hbm],
        out_specs=(vmem,) * 4,
        scratch_shapes=[
            pltpu.VMEM((LEVELS * half, tall), f32),
            pltpu.VMEM((LEVELS, tall, half), f32),
            pltpu.VMEM((LEVELS, wide, 2 * cols), f32),
            pltpu.SemaphoreType.DMA((2 + 2 * LEVELS,)),
        ],
        compiler_params=params,
        name="prepare",
    )(margin, basis_seed.T, energy, kept(jnp.asarray(table)), kept(jnp.asarray(table_t)), kept(jnp.asarray(col_table(cols))))
    rounds = doubling()
    for round_ in rounds[:-1]:
        energy = added(energy, partner(energy, round_), basis)

    above_shape = jax.ShapeDtypeStruct((channels * BORDER + 8, cols), f32)
    strip_shape = jax.ShapeDtypeStruct((channels * 8 + 8, LANES), f32)
    own_part, *parts = pl.pallas_call(
        bank_kernel,
        out_shape=(image_shape, above_shape, strip_shape, strip_shape),
        in_specs=[vmem] * 7 + [anywhere],
        out_specs=(vmem,) * 4,
        scratch_shapes=[pltpu.VMEM((LEVELS, channels, half, wide), bf16) for i in range(4)],
        compiler_params=params,
        name="bank",
    )(own, above, left, corner, a, a_t, g, energy)
    energy, *parts = pl.pallas_call(
        stamp_kernel,
        out_shape=(jax.ShapeDtypeStruct(energy.shape, f32), above_shape, strip_shape, strip_shape),
        in_specs=[vmem] * 5,
        out_specs=(vmem,) * 4,
        input_output_aliases={2: 1, 3: 2, 4: 3},
        compiler_params=pltpu.CompilerParams(vmem_limit_bytes=1024 * 1024),
        name="stamp",
    )(energy, partner(energy, rounds[-1]), *parts)
    below = moved(parts[0], (-1, 0))
    right = moved(parts[1], (0, -1))
    corner_back = moved(parts[2], (-1, -1))

    def last(*refs):
        last_kernel(radius, *refs)

    return pl.pallas_call(
        last,
        out_shape=(image_shape, image_shape),
        in_specs=[vmem] * 9,
        compiler_params=params,
        name="last",
    )(own, shifted, gain, basis, energy, own_part, below, right, corner_back)


def solution(mesh):
    return jax.shard_map(
        per_device,
        mesh=mesh,
        in_specs=(
            P(None, "fy", "fx"),
            P(None, "fy", "fx"),
            P(None, "fy", "fx"),
            P(),
            P("fy", "fx", None, None),
        ),
        out_specs=(P(None, "fy", "fx"), P(None, "fy", "fx")),
        check_vma=False,
    )
```

```python
import math

import jax
import jax.numpy as jnp
import numpy as np
from jax import lax
from jax.experimental import pallas as pl
from jax.experimental.pallas import tpu as pltpu
from jax.sharding import PartitionSpec as P

LEVELS = 2
BORDER = 32
LANES = 128


DAUBECHIES = [
    -0.00011747678400228192,
    0.0006754494059985568,
    -0.0003917403729959771,
    -0.00487035299301066,
    0.008746094047015655,
    0.013981027917015516,
    -0.04408825393106472,
    -0.01736930100202211,
    0.128747426620186,
    0.00047248457399797254,
    -0.2840155429624281,
    -0.015829105256023893,
    0.5853546836548691,
    0.6756307362980128,
    0.3128715909144659,
    0.05441584224308161,
]
DUAL_STEP = 0.5
PRIMAL_STEP = 0.5
CLIP_LEVEL = 0.08
BALL_SCALE = 0.8
NORM_EPS = 1e-06
WEIGHT = 1.0 / math.sqrt(LEVELS)
BAND_STEP = DUAL_STEP * WEIGHT

LOW = [tap / math.sqrt(2.0) for tap in DAUBECHIES]
HIGH = [(-1.0) ** k * LOW[len(LOW) - 1 - k] for k in range(len(LOW))]


def band(taps, extent, dilation):
    matrix = np.zeros((BORDER + extent, extent), np.float32)
    for k, tap in enumerate(taps):
        for i in range(extent):
            matrix[i - k * dilation + BORDER, i] += np.float32(tap)
    return matrix


def row_table(rows):
    return np.concatenate(
        [band(taps, rows, 2**level).T for level in range(LEVELS) for taps in (LOW, HIGH)], axis=0
    )


def col_table(cols):
    table = np.zeros((LEVELS, cols + LANES, 2 * cols), np.float32)
    for level in range(LEVELS):
        for half, taps in enumerate((LOW, HIGH)):
            matrix = band(taps, cols, 2**level)
            table[level, :cols, half * cols : (half + 1) * cols] = matrix[BORDER:]
            table[level, cols : cols + BORDER, half * cols : (half + 1) * cols] = matrix[:BORDER]
    return table


def terms(value):
    high = value.astype(jnp.bfloat16)
    low = (value - high.astype(jnp.float32)).astype(jnp.bfloat16)
    return high, low


def dot(a, b):
    return lax.dot_general(a, b, (((1,), (0,)), ((), ())), preferred_element_type=jnp.float32)


def lane_iota(shape):
    return lax.broadcasted_iota(jnp.int32, shape, len(shape) - 1)


def row_iota(shape):
    return lax.broadcasted_iota(jnp.int32, shape, len(shape) - 2)


def pack_rows(strip, offset):
    groups = strip.shape[0] // 8
    lane = lane_iota((8, LANES))
    packed = None
    for q in range(groups):
        piece = strip[8 * q : 8 * q + 8]
        shift = (BORDER * q - offset) % LANES
        if shift:
            piece = pltpu.roll(piece, shift, 1)
        packed = piece if packed is None else jnp.where(lane >= BORDER * q, piece, packed)
    return packed


def unpack_rows(packed, offset, groups):
    pieces = []
    for q in range(groups):
        shift = (offset - BORDER * q) % LANES
        pieces.append(pltpu.roll(packed, shift, 1) if shift else packed)
    return jnp.concatenate(pieces, axis=0)


def first_kernel(
    start_hbm, dirty_hbm, sampling_hbm, energy_ref, pack_ref, own_ref, gain_ref, shifted_ref, dirty_ref, sems
):
    channels, rows, cols = own_ref.shape
    parts = sems.shape[0]
    size = channels // parts
    copies = []
    for part in range(parts):
        at = pl.ds(part * size, size)
        trio = [
            pltpu.make_async_copy(source.at[at], target.at[at], sems.at[part, k])
            for k, (source, target) in enumerate(
                ((start_hbm, own_ref), (sampling_hbm, gain_ref), (dirty_hbm, dirty_ref))
            )
        ]
        for copy in trio:
            copy.start()
        copies.append(trio)
    total = jnp.zeros((8, cols), jnp.float32)
    for part in range(parts):
        for copy in copies[part]:
            copy.wait()
        for c in range(part * size, (part + 1) * size):
            field = own_ref[c]
            shifted = DUAL_STEP * gain_ref[c] * field - DUAL_STEP * dirty_ref[c]
            shifted_ref[c] = shifted
            square = shifted * shifted
            for q in range(rows // 8):
                total = total + square[8 * q : 8 * q + 8]
            pack_ref[c] = pack_rows(field, cols - BORDER)
    energy_ref[:8] = total


def prepare_kernel(
    margin_ref, seed_ref, after_ref, rows_ref, rows_t_ref, cols_ref,
    basis_ref, a_ref, at_ref, g_ref,
):
    rank, channels = seed_ref.shape
    eye = row_iota((channels, channels)) == lane_iota((channels, channels))
    columns = []
    for r in range(rank):
        row = jnp.broadcast_to(seed_ref[r : r + 1, :], (channels, channels))
        column = jnp.sum(jnp.where(eye, row, 0.0), axis=1, keepdims=True)
        columns.append(jnp.broadcast_to(column, (channels, LANES)))
    for r in range(rank):
        vector = columns[r]
        vector = vector / jnp.sqrt(jnp.sum(vector * vector, axis=0, keepdims=True))
        basis_ref[r] = vector
        for later in range(r + 1, rank):
            along = jnp.sum(vector * columns[later], axis=0, keepdims=True)
            columns[later] = columns[later] - along * vector

    half, tall = rows_ref.shape[0] // LEVELS, rows_ref.shape[1]
    wide, double = cols_ref.shape[1:]
    cols = double // 2
    first_row = lax.axis_index("fy") == 0
    first_col = lax.axis_index("fx") == 0
    position = lane_iota((half, tall)) - BORDER
    position_t = row_iota((tall, half)) - BORDER
    a_parts, at_parts = [], []
    for level in range(LEVELS):
        width = jnp.where(first_row, 0, margin_ref[0, 0, level, 0])
        a_parts.append(jnp.where(position >= -width, rows_ref[level * half : (level + 1) * half], 0.0))
        at_parts.append(jnp.where(position_t >= -width, rows_t_ref[level], 0.0))
    a_high, a_low = terms(jnp.concatenate(a_parts, axis=0))
    a_ref[...] = jnp.concatenate([a_high, a_high, a_low], axis=1)
    at_pairs = [terms(part) for part in at_parts]
    at_ref[...] = jnp.concatenate(
        [pair[0] for pair in at_pairs] * 2 + [pair[1] for pair in at_pairs], axis=1
    )
    at = row_iota((wide, double))
    for level in range(LEVELS):
        width = jnp.where(first_col, 0, margin_ref[0, 0, level, 1])
        g = jnp.where((at < cols) | (at >= cols + BORDER - width), cols_ref[level], 0.0)
        g_high, g_low = terms(g)
        g_ref[level, 0] = g_high
        g_ref[level, 1] = g_low


def dot_t(a, b):
    return lax.dot_general(a, b, (((1,), (1,)), ((), ())), preferred_element_type=jnp.float32)


def rows_kernel(own_ref, above_ref, left_ref, corner_ref, a_ref, after_ref, z_high, z_low):
    channels, rows, cols = own_ref.shape
    groups = rows // 8
    half = 2 * rows
    for c in range(channels):
        upper = jnp.concatenate([above_ref[c], unpack_rows(corner_ref[c], 0, groups)], axis=1)
        lower = jnp.concatenate([own_ref[c], unpack_rows(left_ref[c], 0, groups)], axis=1)
        e_high, e_low = terms(jnp.concatenate([upper, lower], axis=0))
        z = dot(a_ref[...], jnp.concatenate([e_high, e_low, e_high], axis=0))
        part_high, part_low = terms(z)
        for level in range(LEVELS):
            z_high[level, c] = part_high[level * half : (level + 1) * half]
            z_low[level, c] = part_low[level * half : (level + 1) * half]

def bank_kernel(
    z_high, z_low, at_ref, g_ref, own_out, above_out, left_out, corner_out, u_high, u_low,
):
    channels, rows, cols = own_out.shape
    wide = cols + LANES
    half = 2 * rows
    size = channels // 4

    low_rows = row_iota((half, 2 * cols)) < rows
    low_cols = lane_iota((half, 2 * cols)) < cols
    bound = jnp.where(low_rows & low_cols, 0.0, CLIP_LEVEL / BAND_STEP)
    for level in range(LEVELS):
        g_high, g_low = g_ref[level, 0], g_ref[level, 1]
        for start in range(0, channels, size):
            span = slice(start, start + size)
            zh = z_high[level, span].reshape(size * half, wide)
            zl = z_low[level, span].reshape(size * half, wide)
            coef = dot(jnp.concatenate([zh, zl, zh], axis=1), jnp.concatenate([g_high, g_high, g_low], axis=0))
            coef = coef.reshape(size, half, 2 * cols)
            coef = jnp.minimum(jnp.maximum(coef, -bound), bound).reshape(size * half, 2 * cols)
            t_high, t_low = terms(coef)
            u = dot_t(
                jnp.concatenate([t_high, t_low, t_high], axis=1),
                jnp.concatenate([g_high, g_high, g_low], axis=1),
            )
            part_high, part_low = terms(u)
            u_high[level, span] = part_high.reshape(size, half, wide)
            u_low[level, span] = part_low.reshape(size, half, wide)

    for c in range(channels):
        highs = [u_high[level, c] for level in range(LEVELS)]
        lows = [u_low[level, c] for level in range(LEVELS)]
        back = dot(at_ref[...], jnp.concatenate(highs + lows + highs, axis=0))
        above_out[BORDER * c : BORDER * (c + 1)] = back[:BORDER, :cols]
        own_out[c] = back[BORDER:, :cols]
        corner_out[8 * c : 8 * (c + 1)] = pack_rows(back[:BORDER, cols:], 0)
        left_out[8 * c : 8 * (c + 1)] = pack_rows(back[BORDER:, cols:], 0)


def last_kernel(
    radius, start_ref, shifted_ref, sampling_ref, basis_ref, energy_ref, own_ref, below_ref, right_ref, corner_ref,
    image_ref, dual_ref,
):
    channels, rows, cols = start_ref.shape
    rank = basis_ref.shape[0]
    groups = rows // 8
    energy = energy_ref[...]
    for ref in (below_ref, right_ref, corner_ref):
        energy = energy + ref[pl.ds(ref.shape[0] - 8, 8)]
    energy = jnp.sum(jnp.sum(energy, axis=0, keepdims=True), axis=1, keepdims=True)
    factor = jnp.maximum(0.0, 1.0 - DUAL_STEP * radius / jnp.sqrt(energy + NORM_EPS))
    factor = jnp.broadcast_to(factor, (rows, cols))
    edge = lane_iota((rows, cols)) >= cols - BORDER
    weights = [jnp.zeros((rows, cols), jnp.float32) for r in range(rank)]
    for c in range(channels):
        field = start_ref[c]
        gain = sampling_ref[c]
        dual = factor * shifted_ref[c]
        dual_ref[c] = dual
        strip = right_ref[8 * c : 8 * (c + 1)] + corner_ref[8 * c : 8 * (c + 1)]
        strip = unpack_rows(strip, cols - BORDER, groups)
        prior = own_ref[c] + below_ref[BORDER * c : BORDER * (c + 1)] + jnp.where(edge, strip, 0.0)
        stepped = field - PRIMAL_STEP * (gain * dual + (WEIGHT * BAND_STEP) * prior)
        for r in range(rank):
            weights[r] = weights[r] + basis_ref[r, c : c + 1, :] * stepped
    for c in range(channels):
        total = basis_ref[0, c : c + 1, :] * weights[0]
        for r in range(1, rank):
            total = total + basis_ref[r, c : c + 1, :] * weights[r]
        image_ref[c] = jnp.maximum(total, 0.0)


def shift(axis_sizes, steps):
    return [
        (
            a * axis_sizes[1] + b,
            (a + steps[0]) % axis_sizes[0] * axis_sizes[1] + (b + steps[1]) % axis_sizes[1],
        )
        for a in range(axis_sizes[0])
        for b in range(axis_sizes[1])
    ]


def add_kernel(value_ref, arrived_ref, *refs):
    refs[-1][...] = value_ref[:8] + arrived_ref[:8]


def doubling():
    rounds = []
    for axis in ("fy", "fx"):
        step = 2
        while step < lax.axis_size(axis):
            rounds.append((axis, step))
            step *= 2
    return rounds


def partner(value, round_):
    axis, step = round_
    return lax.ppermute(value, axis, [(i, i ^ step) for i in range(lax.axis_size(axis))])


def stamp_kernel(value_ref, arrived_ref, above_in, left_in, corner_in, total_ref, above_ref, left_ref, corner_ref):
    total = value_ref[...] + arrived_ref[...]
    total_ref[...] = total
    for ref in (above_ref, left_ref, corner_ref):
        ref[pl.ds(ref.shape[0] - 8, 8)] = total


def added(value, arrived, *after):
    return pl.pallas_call(
        add_kernel,
        out_shape=jax.ShapeDtypeStruct((8, value.shape[1]), value.dtype),
        in_specs=[pl.BlockSpec(memory_space=pltpu.VMEM)] * 2 + [pl.BlockSpec(memory_space=pl.ANY)] * len(after),
        out_specs=pl.BlockSpec(memory_space=pltpu.VMEM),
        compiler_params=pltpu.CompilerParams(vmem_limit_bytes=1024 * 1024),
        name="add",
    )(value, arrived, *after)


def per_device(start_image, dirty, sampling, basis_seed, margin):
    channels, rows, cols = start_image.shape
    rank = basis_seed.shape[1]
    sizes = (lax.axis_size("fy"), lax.axis_size("fx"))
    half = 2 * rows
    tall = rows + BORDER
    wide = cols + LANES
    radius = BALL_SCALE * math.sqrt(channels * rows * cols * sizes[0] * sizes[1])
    f32, bf16 = jnp.float32, jnp.bfloat16
    image_shape = jax.ShapeDtypeStruct((channels, rows, cols), f32)
    pack_shape = jax.ShapeDtypeStruct((channels, 8, LANES), f32)
    params = pltpu.CompilerParams(vmem_limit_bytes=16 * 1024 * 1024)
    vmem = pl.BlockSpec(memory_space=pltpu.VMEM)
    smem = pl.BlockSpec(memory_space=pltpu.SMEM)
    hbm = pl.BlockSpec(memory_space=pltpu.HBM)
    anywhere = pl.BlockSpec(memory_space=pl.ANY)

    def kept(value):
        return pltpu.with_memory_space_constraint(value, pltpu.HBM)

    def moved(value, steps):
        return lax.ppermute(value, ("fy", "fx"), shift(sizes, steps))

    above = moved(start_image, (1, 0))
    energy, pack, own, gain, shifted = pl.pallas_call(
        first_kernel,
        out_shape=(jax.ShapeDtypeStruct((128, cols), f32), pack_shape, image_shape, image_shape, image_shape),
        in_specs=[hbm] * 3,
        out_specs=(vmem,) * 5,
        scratch_shapes=[pltpu.VMEM((channels, rows, cols), f32), pltpu.SemaphoreType.DMA((4, 3))],
        compiler_params=params,
        name="first",
    )(kept(start_image), kept(dirty), kept(sampling))
    left = moved(pack, (0, 1))
    corner = moved(pack, (1, 1))

    rounds = doubling()
    energy = added(energy, partner(energy, rounds[0]))

    table = row_table(rows)
    table_t = np.ascontiguousarray(table.reshape(LEVELS, half, tall).transpose(0, 2, 1))
    basis, a, a_t, g = pl.pallas_call(
        prepare_kernel,
        out_shape=(
            jax.ShapeDtypeStruct((rank, channels, LANES), f32),
            jax.ShapeDtypeStruct((LEVELS * half, 3 * tall), bf16),
            jax.ShapeDtypeStruct((tall, 3 * LEVELS * half), bf16),
            jax.ShapeDtypeStruct((LEVELS, 2, wide, 2 * cols), bf16),
        ),
        in_specs=[smem, vmem, anywhere, vmem, vmem, vmem],
        out_specs=(vmem,) * 4,
        compiler_params=params,
        name="prepare",
    )(margin, basis_seed.T, energy, table, table_t, col_table(cols))
    for round_ in rounds[1:-1]:
        energy = added(energy, partner(energy, round_), basis)
    arriving = partner(energy, rounds[-1])
    bank_shape = jax.ShapeDtypeStruct((LEVELS, channels, half, wide), bf16)
    z_high, z_low = pl.pallas_call(
        rows_kernel,
        out_shape=(bank_shape, bank_shape),
        in_specs=[vmem] * 5 + [anywhere],
        out_specs=(vmem,) * 2,
        compiler_params=params,
        name="rows",
    )(own, above, left, corner, a, energy)

    above_shape = jax.ShapeDtypeStruct((channels * BORDER + 8, cols), f32)
    strip_shape = jax.ShapeDtypeStruct((channels * 8 + 8, LANES), f32)
    own_part, *parts = pl.pallas_call(
        bank_kernel,
        out_shape=(image_shape, above_shape, strip_shape, strip_shape),
        in_specs=[vmem] * 4,
        out_specs=(vmem,) * 4,
        scratch_shapes=[pltpu.VMEM(bank_shape.shape, bf16)] * 2,
        compiler_params=params,
        name="bank",
    )(z_high, z_low, a_t, g)
    energy, *parts = pl.pallas_call(
        stamp_kernel,
        out_shape=(jax.ShapeDtypeStruct(energy.shape, f32), above_shape, strip_shape, strip_shape),
        in_specs=[vmem] * 5,
        out_specs=(vmem,) * 4,
        input_output_aliases={2: 1, 3: 2, 4: 3},
        compiler_params=pltpu.CompilerParams(vmem_limit_bytes=1024 * 1024),
        name="stamp",
    )(energy, arriving, *parts)
    below = moved(parts[0], (-1, 0))
    right = moved(parts[1], (0, -1))
    corner_back = moved(parts[2], (-1, -1))

    def last(*refs):
        last_kernel(radius, *refs)

    return pl.pallas_call(
        last,
        out_shape=(image_shape, image_shape),
        in_specs=[vmem] * 9,
        compiler_params=params,
        name="last",
    )(own, shifted, gain, basis, energy, own_part, below, right, corner_back)


def solution(mesh):
    return jax.shard_map(
        per_device,
        mesh=mesh,
        in_specs=(
            P(None, "fy", "fx"),
            P(None, "fy", "fx"),
            P(None, "fy", "fx"),
            P(),
            P("fy", "fx", None, None),
        ),
        out_specs=(P(None, "fy", "fx"), P(None, "fy", "fx")),
        check_vma=False,
    )
```

```python
import math

import jax
import jax.numpy as jnp
import numpy as np
from jax import lax
from jax.experimental import pallas as pl
from jax.experimental.pallas import tpu as pltpu
from jax.sharding import PartitionSpec as P

LEVELS = 2
BORDER = 32
LANES = 128


DAUBECHIES = [
    -0.00011747678400228192,
    0.0006754494059985568,
    -0.0003917403729959771,
    -0.00487035299301066,
    0.008746094047015655,
    0.013981027917015516,
    -0.04408825393106472,
    -0.01736930100202211,
    0.128747426620186,
    0.00047248457399797254,
    -0.2840155429624281,
    -0.015829105256023893,
    0.5853546836548691,
    0.6756307362980128,
    0.3128715909144659,
    0.05441584224308161,
]
DUAL_STEP = 0.5
PRIMAL_STEP = 0.5
CLIP_LEVEL = 0.08
BALL_SCALE = 0.8
NORM_EPS = 1e-06
WEIGHT = 1.0 / math.sqrt(LEVELS)
BAND_STEP = DUAL_STEP * WEIGHT

LOW = [tap / math.sqrt(2.0) for tap in DAUBECHIES]
HIGH = [(-1.0) ** k * LOW[len(LOW) - 1 - k] for k in range(len(LOW))]


def band(taps, extent, dilation):
    matrix = np.zeros((BORDER + extent, extent), np.float32)
    for k, tap in enumerate(taps):
        for i in range(extent):
            matrix[i - k * dilation + BORDER, i] += np.float32(tap)
    return matrix


def row_table(rows):
    return np.concatenate(
        [band(taps, rows, 2**level).T for level in range(LEVELS) for taps in (LOW, HIGH)], axis=0
    )


def col_table(cols):
    table = np.zeros((LEVELS, cols + LANES, 2 * cols), np.float32)
    for level in range(LEVELS):
        for half, taps in enumerate((LOW, HIGH)):
            matrix = band(taps, cols, 2**level)
            table[level, :cols, half * cols : (half + 1) * cols] = matrix[BORDER:]
            table[level, cols : cols + BORDER, half * cols : (half + 1) * cols] = matrix[:BORDER]
    return table


def terms(value):
    high = value.astype(jnp.bfloat16)
    low = (value - high.astype(jnp.float32)).astype(jnp.bfloat16)
    return high, low


def dot(a, b):
    return lax.dot_general(a, b, (((1,), (0,)), ((), ())), preferred_element_type=jnp.float32)


def lane_iota(shape):
    return lax.broadcasted_iota(jnp.int32, shape, len(shape) - 1)


def row_iota(shape):
    return lax.broadcasted_iota(jnp.int32, shape, len(shape) - 2)


def pack_rows(strip, offset):
    groups = strip.shape[0] // 8
    lane = lane_iota((8, LANES))
    packed = None
    for q in range(groups):
        piece = strip[8 * q : 8 * q + 8]
        shift = (BORDER * q - offset) % LANES
        if shift:
            piece = pltpu.roll(piece, shift, 1)
        packed = piece if packed is None else jnp.where(lane >= BORDER * q, piece, packed)
    return packed


def unpack_rows(packed, offset, groups):
    pieces = []
    for q in range(groups):
        shift = (offset - BORDER * q) % LANES
        pieces.append(pltpu.roll(packed, shift, 1) if shift else packed)
    return jnp.concatenate(pieces, axis=0)


def first_kernel(
    start_hbm, dirty_hbm, sampling_hbm, energy_ref, pack_ref, own_ref, gain_ref, shifted_ref, dirty_ref, sems
):
    channels, rows, cols = own_ref.shape
    parts = sems.shape[0]
    size = channels // parts
    copies = []
    for part in range(parts):
        at = pl.ds(part * size, size)
        trio = [
            pltpu.make_async_copy(source.at[at], target.at[at], sems.at[part, k])
            for k, (source, target) in enumerate(
                ((start_hbm, own_ref), (sampling_hbm, gain_ref), (dirty_hbm, dirty_ref))
            )
        ]
        for copy in trio:
            copy.start()
        copies.append(trio)
    total = jnp.zeros((8, cols), jnp.float32)
    for part in range(parts):
        for copy in copies[part]:
            copy.wait()
        for c in range(part * size, (part + 1) * size):
            field = own_ref[c]
            shifted = DUAL_STEP * gain_ref[c] * field - DUAL_STEP * dirty_ref[c]
            shifted_ref[c] = shifted
            square = shifted * shifted
            for q in range(rows // 8):
                total = total + square[8 * q : 8 * q + 8]
            pack_ref[c] = pack_rows(field, cols - BORDER)
    energy_ref[:8] = total


def prepare_kernel(
    margin_ref, seed_ref, after_ref, rows_ref, rows_t_ref, cols_ref,
    basis_ref, a_ref, at_ref, g_ref,
):
    rank, channels = seed_ref.shape
    eye = row_iota((channels, channels)) == lane_iota((channels, channels))
    columns = []
    for r in range(rank):
        row = jnp.broadcast_to(seed_ref[r : r + 1, :], (channels, channels))
        column = jnp.sum(jnp.where(eye, row, 0.0), axis=1, keepdims=True)
        columns.append(jnp.broadcast_to(column, (channels, LANES)))
    for r in range(rank):
        vector = columns[r]
        vector = vector / jnp.sqrt(jnp.sum(vector * vector, axis=0, keepdims=True))
        basis_ref[r] = vector
        for later in range(r + 1, rank):
            along = jnp.sum(vector * columns[later], axis=0, keepdims=True)
            columns[later] = columns[later] - along * vector

    half, tall = rows_ref.shape[0] // LEVELS, rows_ref.shape[1]
    wide, double = cols_ref.shape[1:]
    cols = double // 2
    first_row = lax.axis_index("fy") == 0
    first_col = lax.axis_index("fx") == 0
    position = lane_iota((half, tall)) - BORDER
    position_t = row_iota((tall, half)) - BORDER
    a_parts, at_parts = [], []
    for level in range(LEVELS):
        width = jnp.where(first_row, 0, margin_ref[0, 0, level, 0])
        a_parts.append(jnp.where(position >= -width, rows_ref[level * half : (level + 1) * half], 0.0))
        at_parts.append(jnp.where(position_t >= -width, rows_t_ref[level], 0.0))
    a_high, a_low = terms(jnp.concatenate(a_parts, axis=0))
    a_ref[...] = jnp.concatenate([a_high, a_high, a_low], axis=1)
    at_pairs = [terms(part) for part in at_parts]
    at_ref[...] = jnp.concatenate(
        [pair[0] for pair in at_pairs] * 2 + [pair[1] for pair in at_pairs], axis=1
    )
    at = row_iota((wide, double))
    for level in range(LEVELS):
        width = jnp.where(first_col, 0, margin_ref[0, 0, level, 1])
        g = jnp.where((at < cols) | (at >= cols + BORDER - width), cols_ref[level], 0.0)
        g_high, g_low = terms(g)
        g_ref[level, 0] = g_high
        g_ref[level, 1] = g_low


def dot_t(a, b):
    return lax.dot_general(a, b, (((1,), (1,)), ((), ())), preferred_element_type=jnp.float32)


def rows_kernel(own_ref, above_ref, left_ref, corner_ref, a_ref, after_ref, z_high, z_low):
    channels, rows, cols = own_ref.shape
    groups = rows // 8
    half = 2 * rows
    for c in range(channels):
        upper = jnp.concatenate([above_ref[c], unpack_rows(corner_ref[c], 0, groups)], axis=1)
        lower = jnp.concatenate([own_ref[c], unpack_rows(left_ref[c], 0, groups)], axis=1)
        e_high, e_low = terms(jnp.concatenate([upper, lower], axis=0))
        z = dot(a_ref[...], jnp.concatenate([e_high, e_low, e_high], axis=0))
        part_high, part_low = terms(z)
        for level in range(LEVELS):
            z_high[level, c] = part_high[level * half : (level + 1) * half]
            z_low[level, c] = part_low[level * half : (level + 1) * half]

def bank_kernel(
    z_high, z_low, at_ref, g_ref, own_out, above_out, left_out, corner_out, u_high, u_low,
):
    channels, rows, cols = own_out.shape
    wide = cols + LANES
    half = 2 * rows
    size = channels // 4

    low_rows = row_iota((half, 2 * cols)) < rows
    low_cols = lane_iota((half, 2 * cols)) < cols
    bound = jnp.where(low_rows & low_cols, 0.0, CLIP_LEVEL / BAND_STEP)
    for level in range(LEVELS):
        g_high, g_low = g_ref[level, 0], g_ref[level, 1]
        for start in range(0, channels, size):
            span = slice(start, start + size)
            zh = z_high[level, span].reshape(size * half, wide)
            zl = z_low[level, span].reshape(size * half, wide)
            coef = dot(jnp.concatenate([zh, zl, zh], axis=1), jnp.concatenate([g_high, g_high, g_low], axis=0))
            coef = coef.reshape(size, half, 2 * cols)
            coef = jnp.minimum(jnp.maximum(coef, -bound), bound).reshape(size * half, 2 * cols)
            t_high, t_low = terms(coef)
            u = dot_t(
                jnp.concatenate([t_high, t_low, t_high], axis=1),
                jnp.concatenate([g_high, g_high, g_low], axis=1),
            )
            part_high, part_low = terms(u)
            u_high[level, span] = part_high.reshape(size, half, wide)
            u_low[level, span] = part_low.reshape(size, half, wide)

    for c in range(channels):
        highs = [u_high[level, c] for level in range(LEVELS)]
        lows = [u_low[level, c] for level in range(LEVELS)]
        back = dot(at_ref[...], jnp.concatenate(highs + lows + highs, axis=0))
        above_out[BORDER * c : BORDER * (c + 1)] = back[:BORDER, :cols]
        own_out[c] = back[BORDER:, :cols]
        corner_out[8 * c : 8 * (c + 1)] = pack_rows(back[:BORDER, cols:], 0)
        left_out[8 * c : 8 * (c + 1)] = pack_rows(back[BORDER:, cols:], 0)


def begin_kernel(own_ref, shifted_ref, gain_ref, basis_ref, part_ref, after_ref, plain_ref, scaled_ref):
    channels, rows, cols = own_ref.shape
    rank = basis_ref.shape[0]
    plain = [jnp.zeros((rows, cols), jnp.float32) for r in range(rank)]
    scaled = [jnp.zeros((rows, cols), jnp.float32) for r in range(rank)]
    for c in range(channels):
        first = own_ref[c] - (PRIMAL_STEP * WEIGHT * BAND_STEP) * part_ref[c]
        second = PRIMAL_STEP * gain_ref[c] * shifted_ref[c]
        for r in range(rank):
            plain[r] = plain[r] + basis_ref[r, c : c + 1, :] * first
            scaled[r] = scaled[r] + basis_ref[r, c : c + 1, :] * second
    for r in range(rank):
        plain_ref[r] = plain[r]
        scaled_ref[r] = scaled[r]


def last_kernel(
    radius, shifted_ref, basis_ref, energy_ref, plain_ref, scaled_ref, below_ref, right_ref, corner_ref,
    image_ref, dual_ref,
):
    channels, rows, cols = shifted_ref.shape
    rank = basis_ref.shape[0]
    groups = rows // 8
    energy = energy_ref[...]
    for ref in (below_ref, right_ref, corner_ref):
        energy = energy + ref[pl.ds(ref.shape[0] - 8, 8)]
    energy = jnp.sum(jnp.sum(energy, axis=0, keepdims=True), axis=1, keepdims=True)
    factor = jnp.maximum(0.0, 1.0 - DUAL_STEP * radius / jnp.sqrt(energy + NORM_EPS))
    factor = jnp.broadcast_to(factor, (rows, cols))
    edge = lane_iota((rows, cols)) >= cols - BORDER
    weights = [jnp.zeros((rows, cols), jnp.float32) for r in range(rank)]
    for c in range(channels):
        dual_ref[c] = factor * shifted_ref[c]
        strip = right_ref[8 * c : 8 * (c + 1)] + corner_ref[8 * c : 8 * (c + 1)]
        strip = unpack_rows(strip, cols - BORDER, groups)
        prior = below_ref[BORDER * c : BORDER * (c + 1)] + jnp.where(edge, strip, 0.0)
        for r in range(rank):
            weights[r] = weights[r] + basis_ref[r, c : c + 1, :] * prior
    for r in range(rank):
        weights[r] = (plain_ref[r] - factor * scaled_ref[r]) - (PRIMAL_STEP * WEIGHT * BAND_STEP) * weights[r]
    for c in range(channels):
        total = basis_ref[0, c : c + 1, :] * weights[0]
        for r in range(1, rank):
            total = total + basis_ref[r, c : c + 1, :] * weights[r]
        image_ref[c] = jnp.maximum(total, 0.0)


def shift(axis_sizes, steps):
    return [
        (
            a * axis_sizes[1] + b,
            (a + steps[0]) % axis_sizes[0] * axis_sizes[1] + (b + steps[1]) % axis_sizes[1],
        )
        for a in range(axis_sizes[0])
        for b in range(axis_sizes[1])
    ]


def add_kernel(value_ref, arrived_ref, *refs):
    refs[-1][...] = value_ref[:8] + arrived_ref[:8]


def doubling():
    rounds = []
    for axis in ("fy", "fx"):
        step = 2
        while step < lax.axis_size(axis):
            rounds.append((axis, step))
            step *= 2
    return rounds


def partner(value, round_):
    axis, step = round_
    return lax.ppermute(value, axis, [(i, i ^ step) for i in range(lax.axis_size(axis))])


def stamp_kernel(value_ref, arrived_ref, above_in, left_in, corner_in, total_ref, above_ref, left_ref, corner_ref):
    total = value_ref[...] + arrived_ref[...]
    total_ref[...] = total
    for ref in (above_ref, left_ref, corner_ref):
        ref[pl.ds(ref.shape[0] - 8, 8)] = total


def added(value, arrived, *after):
    return pl.pallas_call(
        add_kernel,
        out_shape=jax.ShapeDtypeStruct((8, value.shape[1]), value.dtype),
        in_specs=[pl.BlockSpec(memory_space=pltpu.VMEM)] * 2 + [pl.BlockSpec(memory_space=pl.ANY)] * len(after),
        out_specs=pl.BlockSpec(memory_space=pltpu.VMEM),
        compiler_params=pltpu.CompilerParams(vmem_limit_bytes=1024 * 1024),
        name="add",
    )(value, arrived, *after)


def per_device(start_image, dirty, sampling, basis_seed, margin):
    channels, rows, cols = start_image.shape
    rank = basis_seed.shape[1]
    sizes = (lax.axis_size("fy"), lax.axis_size("fx"))
    half = 2 * rows
    tall = rows + BORDER
    wide = cols + LANES
    radius = BALL_SCALE * math.sqrt(channels * rows * cols * sizes[0] * sizes[1])
    f32, bf16 = jnp.float32, jnp.bfloat16
    image_shape = jax.ShapeDtypeStruct((channels, rows, cols), f32)
    pack_shape = jax.ShapeDtypeStruct((channels, 8, LANES), f32)
    params = pltpu.CompilerParams(vmem_limit_bytes=16 * 1024 * 1024)
    vmem = pl.BlockSpec(memory_space=pltpu.VMEM)
    smem = pl.BlockSpec(memory_space=pltpu.SMEM)
    hbm = pl.BlockSpec(memory_space=pltpu.HBM)
    anywhere = pl.BlockSpec(memory_space=pl.ANY)

    def kept(value):
        return pltpu.with_memory_space_constraint(value, pltpu.HBM)

    def moved(value, steps):
        return lax.ppermute(value, ("fy", "fx"), shift(sizes, steps))

    above = moved(start_image, (1, 0))
    energy, pack, own, gain, shifted = pl.pallas_call(
        first_kernel,
        out_shape=(jax.ShapeDtypeStruct((128, cols), f32), pack_shape, image_shape, image_shape, image_shape),
        in_specs=[hbm] * 3,
        out_specs=(vmem,) * 5,
        scratch_shapes=[pltpu.VMEM((channels, rows, cols), f32), pltpu.SemaphoreType.DMA((1, 3))],
        compiler_params=params,
        name="first",
    )(kept(start_image), kept(dirty), kept(sampling))
    left = moved(pack, (0, 1))
    corner = moved(pack, (1, 1))

    rounds = doubling()
    energy = added(energy, partner(energy, rounds[0]))

    table = row_table(rows)
    table_t = np.ascontiguousarray(table.reshape(LEVELS, half, tall).transpose(0, 2, 1))
    basis, a, a_t, g = pl.pallas_call(
        prepare_kernel,
        out_shape=(
            jax.ShapeDtypeStruct((rank, channels, LANES), f32),
            jax.ShapeDtypeStruct((LEVELS * half, 3 * tall), bf16),
            jax.ShapeDtypeStruct((tall, 3 * LEVELS * half), bf16),
            jax.ShapeDtypeStruct((LEVELS, 2, wide, 2 * cols), bf16),
        ),
        in_specs=[smem, vmem, anywhere, vmem, vmem, vmem],
        out_specs=(vmem,) * 4,
        compiler_params=params,
        name="prepare",
    )(margin, basis_seed.T, energy, table, table_t, col_table(cols))
    for round_ in rounds[1:-1]:
        energy = added(energy, partner(energy, round_), basis)
    arriving = partner(energy, rounds[-1])
    bank_shape = jax.ShapeDtypeStruct((LEVELS, channels, half, wide), bf16)
    z_high, z_low = pl.pallas_call(
        rows_kernel,
        out_shape=(bank_shape, bank_shape),
        in_specs=[vmem] * 5 + [anywhere],
        out_specs=(vmem,) * 2,
        compiler_params=params,
        name="rows",
    )(own, above, left, corner, a, energy)

    above_shape = jax.ShapeDtypeStruct((channels * BORDER + 8, cols), f32)
    strip_shape = jax.ShapeDtypeStruct((channels * 8 + 8, LANES), f32)
    own_part, *parts = pl.pallas_call(
        bank_kernel,
        out_shape=(image_shape, above_shape, strip_shape, strip_shape),
        in_specs=[vmem] * 4,
        out_specs=(vmem,) * 4,
        scratch_shapes=[pltpu.VMEM(bank_shape.shape, bf16)] * 2,
        compiler_params=params,
        name="bank",
    )(z_high, z_low, a_t, g)
    energy, *parts = pl.pallas_call(
        stamp_kernel,
        out_shape=(jax.ShapeDtypeStruct(energy.shape, f32), above_shape, strip_shape, strip_shape),
        in_specs=[vmem] * 5,
        out_specs=(vmem,) * 4,
        input_output_aliases={2: 1, 3: 2, 4: 3},
        compiler_params=pltpu.CompilerParams(vmem_limit_bytes=1024 * 1024),
        name="stamp",
    )(energy, arriving, *parts)
    below = moved(parts[0], (-1, 0))
    right = moved(parts[1], (0, -1))
    corner_back = moved(parts[2], (-1, -1))

    weight_shape = jax.ShapeDtypeStruct((rank, rows, cols), f32)
    plain, scaled = pl.pallas_call(
        begin_kernel,
        out_shape=(weight_shape, weight_shape),
        in_specs=[vmem] * 5 + [anywhere],
        out_specs=(vmem,) * 2,
        compiler_params=params,
        name="begin",
    )(own, shifted, gain, basis, own_part, energy)

    def last(*refs):
        last_kernel(radius, *refs)

    return pl.pallas_call(
        last,
        out_shape=(image_shape, image_shape),
        in_specs=[vmem] * 8,
        compiler_params=params,
        name="last",
    )(shifted, basis, energy, plain, scaled, below, right, corner_back)


def solution(mesh):
    return jax.shard_map(
        per_device,
        mesh=mesh,
        in_specs=(
            P(None, "fy", "fx"),
            P(None, "fy", "fx"),
            P(None, "fy", "fx"),
            P(),
            P("fy", "fx", None, None),
        ),
        out_specs=(P(None, "fy", "fx"), P(None, "fy", "fx")),
        check_vma=False,
    )
```

```python
import math

import jax
import jax.numpy as jnp
import numpy as np
from jax import lax
from jax.experimental import pallas as pl
from jax.experimental.pallas import tpu as pltpu
from jax.sharding import PartitionSpec as P

LEVELS = 2
BORDER = 32
LANES = 128


DAUBECHIES = [
    -0.00011747678400228192,
    0.0006754494059985568,
    -0.0003917403729959771,
    -0.00487035299301066,
    0.008746094047015655,
    0.013981027917015516,
    -0.04408825393106472,
    -0.01736930100202211,
    0.128747426620186,
    0.00047248457399797254,
    -0.2840155429624281,
    -0.015829105256023893,
    0.5853546836548691,
    0.6756307362980128,
    0.3128715909144659,
    0.05441584224308161,
]
DUAL_STEP = 0.5
PRIMAL_STEP = 0.5
CLIP_LEVEL = 0.08
BALL_SCALE = 0.8
NORM_EPS = 1e-06
AHEAD = pl.CostEstimate(flops=10**9, transcendentals=0, bytes_accessed=10**8)
WEIGHT = 1.0 / math.sqrt(LEVELS)
BAND_STEP = DUAL_STEP * WEIGHT

LOW = [tap / math.sqrt(2.0) for tap in DAUBECHIES]
HIGH = [(-1.0) ** k * LOW[len(LOW) - 1 - k] for k in range(len(LOW))]


def band(taps, extent, dilation):
    matrix = np.zeros((BORDER + extent, extent), np.float32)
    for k, tap in enumerate(taps):
        for i in range(extent):
            matrix[i - k * dilation + BORDER, i] += np.float32(tap)
    return matrix


def row_table(rows):
    return np.concatenate(
        [band(taps, rows, 2**level).T for level in range(LEVELS) for taps in (LOW, HIGH)], axis=0
    )


def col_table(cols):
    table = np.zeros((LEVELS, cols + LANES, 2 * cols), np.float32)
    for level in range(LEVELS):
        for half, taps in enumerate((LOW, HIGH)):
            matrix = band(taps, cols, 2**level)
            table[level, :cols, half * cols : (half + 1) * cols] = matrix[BORDER:]
            table[level, cols : cols + BORDER, half * cols : (half + 1) * cols] = matrix[:BORDER]
    return table


def terms(value):
    high = value.astype(jnp.bfloat16)
    low = (value - high.astype(jnp.float32)).astype(jnp.bfloat16)
    return high, low


def dot(a, b):
    return lax.dot_general(a, b, (((1,), (0,)), ((), ())), preferred_element_type=jnp.float32)


def lane_iota(shape):
    return lax.broadcasted_iota(jnp.int32, shape, len(shape) - 1)


def row_iota(shape):
    return lax.broadcasted_iota(jnp.int32, shape, len(shape) - 2)


def pack_rows(strip, offset):
    groups = strip.shape[0] // 8
    lane = lane_iota((8, LANES))
    packed = None
    for q in range(groups):
        piece = strip[8 * q : 8 * q + 8]
        shift = (BORDER * q - offset) % LANES
        if shift:
            piece = pltpu.roll(piece, shift, 1)
        packed = piece if packed is None else jnp.where(lane >= BORDER * q, piece, packed)
    return packed


def unpack_rows(packed, offset, groups):
    pieces = []
    for q in range(groups):
        shift = (offset - BORDER * q) % LANES
        pieces.append(pltpu.roll(packed, shift, 1) if shift else packed)
    return jnp.concatenate(pieces, axis=0)


def first_kernel(
    start_hbm, dirty_hbm, sampling_hbm, energy_ref, pack_ref, own_ref, gain_ref, shifted_ref, dirty_ref, sems
):
    channels, rows, cols = own_ref.shape
    parts = sems.shape[0]
    size = channels // parts
    copies = []
    for part in range(parts):
        at = pl.ds(part * size, size)
        trio = [
            pltpu.make_async_copy(source.at[at], target.at[at], sems.at[part, k])
            for k, (source, target) in enumerate(
                ((start_hbm, own_ref), (sampling_hbm, gain_ref), (dirty_hbm, dirty_ref))
            )
        ]
        for copy in trio:
            copy.start()
        copies.append(trio)
    total = jnp.zeros((8, cols), jnp.float32)
    for part in range(parts):
        for copy in copies[part]:
            copy.wait()
        for c in range(part * size, (part + 1) * size):
            field = own_ref[c]
            shifted = DUAL_STEP * gain_ref[c] * field - DUAL_STEP * dirty_ref[c]
            shifted_ref[c] = shifted
            square = shifted * shifted
            for q in range(rows // 8):
                total = total + square[8 * q : 8 * q + 8]
            pack_ref[c] = pack_rows(field, cols - BORDER)
    energy_ref[:8] = total


def prepare_kernel(
    margin_ref, seed_ref, after_ref, rows_ref, rows_t_ref, cols_ref,
    basis_ref, a_ref, at_ref, g_ref,
):
    rank, channels = seed_ref.shape
    eye = row_iota((channels, channels)) == lane_iota((channels, channels))
    columns = []
    for r in range(rank):
        row = jnp.broadcast_to(seed_ref[r : r + 1, :], (channels, channels))
        column = jnp.sum(jnp.where(eye, row, 0.0), axis=1, keepdims=True)
        columns.append(jnp.broadcast_to(column, (channels, LANES)))
    for r in range(rank):
        vector = columns[r]
        vector = vector / jnp.sqrt(jnp.sum(vector * vector, axis=0, keepdims=True))
        basis_ref[r] = vector
        for later in range(r + 1, rank):
            along = jnp.sum(vector * columns[later], axis=0, keepdims=True)
            columns[later] = columns[later] - along * vector

    half, tall = rows_ref.shape[0] // LEVELS, rows_ref.shape[1]
    wide, double = cols_ref.shape[1:]
    cols = double // 2
    first_row = lax.axis_index("fy") == 0
    first_col = lax.axis_index("fx") == 0
    position = lane_iota((half, tall)) - BORDER
    position_t = row_iota((tall, half)) - BORDER
    a_parts, at_parts = [], []
    for level in range(LEVELS):
        width = jnp.where(first_row, 0, margin_ref[0, 0, level, 0])
        a_parts.append(jnp.where(position >= -width, rows_ref[level * half : (level + 1) * half], 0.0))
        at_parts.append(jnp.where(position_t >= -width, rows_t_ref[level], 0.0))
    a_high, a_low = terms(jnp.concatenate(a_parts, axis=0))
    a_ref[...] = jnp.concatenate([a_high, a_high, a_low], axis=1)
    at_pairs = [terms(part) for part in at_parts]
    at_ref[...] = jnp.concatenate(
        [pair[0] for pair in at_pairs] * 2 + [pair[1] for pair in at_pairs], axis=1
    )
    at = row_iota((wide, double))
    for level in range(LEVELS):
        width = jnp.where(first_col, 0, margin_ref[0, 0, level, 1])
        g = jnp.where((at < cols) | (at >= cols + BORDER - width), cols_ref[level], 0.0)
        g_high, g_low = terms(g)
        g_ref[level, 0] = g_high
        g_ref[level, 1] = g_low


def dot_t(a, b):
    return lax.dot_general(a, b, (((1,), (1,)), ((), ())), preferred_element_type=jnp.float32)


def rows_kernel(own_ref, above_ref, left_ref, corner_ref, a_ref, after_ref, z_high, z_low):
    channels, rows, cols = own_ref.shape
    groups = rows // 8
    half = 2 * rows
    for c in range(channels):
        upper = jnp.concatenate([above_ref[c], unpack_rows(corner_ref[c], 0, groups)], axis=1)
        lower = jnp.concatenate([own_ref[c], unpack_rows(left_ref[c], 0, groups)], axis=1)
        e_high, e_low = terms(jnp.concatenate([upper, lower], axis=0))
        z = dot(a_ref[...], jnp.concatenate([e_high, e_low, e_high], axis=0))
        part_high, part_low = terms(z)
        for level in range(LEVELS):
            z_high[level, c] = part_high[level * half : (level + 1) * half]
            z_low[level, c] = part_low[level * half : (level + 1) * half]

def bank_kernel(
    z_high, z_low, at_ref, g_ref, own_out, above_out, left_out, corner_out, u_high, u_low,
):
    channels, rows, cols = own_out.shape
    wide = cols + LANES
    half = 2 * rows
    size = channels // 4

    low_rows = row_iota((half, 2 * cols)) < rows
    low_cols = lane_iota((half, 2 * cols)) < cols
    bound = jnp.where(low_rows & low_cols, 0.0, CLIP_LEVEL / BAND_STEP)
    for level in range(LEVELS):
        g_high, g_low = g_ref[level, 0], g_ref[level, 1]
        for start in range(0, channels, size):
            span = slice(start, start + size)
            zh = z_high[level, span].reshape(size * half, wide)
            zl = z_low[level, span].reshape(size * half, wide)
            coef = dot(jnp.concatenate([zh, zl, zh], axis=1), jnp.concatenate([g_high, g_high, g_low], axis=0))
            coef = coef.reshape(size, half, 2 * cols)
            coef = jnp.minimum(jnp.maximum(coef, -bound), bound).reshape(size * half, 2 * cols)
            t_high, t_low = terms(coef)
            u = dot_t(
                jnp.concatenate([t_high, t_low, t_high], axis=1),
                jnp.concatenate([g_high, g_high, g_low], axis=1),
            )
            part_high, part_low = terms(u)
            u_high[level, span] = part_high.reshape(size, half, wide)
            u_low[level, span] = part_low.reshape(size, half, wide)

    for c in range(channels):
        highs = [u_high[level, c] for level in range(LEVELS)]
        lows = [u_low[level, c] for level in range(LEVELS)]
        back = dot(at_ref[...], jnp.concatenate(highs + lows + highs, axis=0))
        above_out[BORDER * c : BORDER * (c + 1)] = back[:BORDER, :cols]
        own_out[c] = back[BORDER:, :cols]
        corner_out[8 * c : 8 * (c + 1)] = pack_rows(back[:BORDER, cols:], 0)
        left_out[8 * c : 8 * (c + 1)] = pack_rows(back[BORDER:, cols:], 0)


def begin_kernel(own_ref, shifted_ref, gain_ref, basis_ref, part_ref, after_ref, plain_ref, scaled_ref):
    channels, rows, cols = own_ref.shape
    rank = basis_ref.shape[0]
    plain = [jnp.zeros((rows, cols), jnp.float32) for r in range(rank)]
    scaled = [jnp.zeros((rows, cols), jnp.float32) for r in range(rank)]
    for c in range(channels):
        first = own_ref[c] - (PRIMAL_STEP * WEIGHT * BAND_STEP) * part_ref[c]
        second = PRIMAL_STEP * gain_ref[c] * shifted_ref[c]
        for r in range(rank):
            plain[r] = plain[r] + basis_ref[r, c : c + 1, :] * first
            scaled[r] = scaled[r] + basis_ref[r, c : c + 1, :] * second
    for r in range(rank):
        plain_ref[r] = plain[r]
        scaled_ref[r] = scaled[r]


def last_kernel(
    radius, shifted_ref, basis_ref, energy_ref, plain_ref, scaled_ref, below_ref, right_ref, corner_ref,
    image_ref, dual_ref,
):
    channels, rows, cols = shifted_ref.shape
    rank = basis_ref.shape[0]
    groups = rows // 8
    energy = energy_ref[...]
    for ref in (below_ref, right_ref, corner_ref):
        energy = energy + ref[pl.ds(ref.shape[0] - 8, 8)]
    energy = jnp.sum(jnp.sum(energy, axis=0, keepdims=True), axis=1, keepdims=True)
    factor = jnp.maximum(0.0, 1.0 - DUAL_STEP * radius / jnp.sqrt(energy + NORM_EPS))
    factor = jnp.broadcast_to(factor, (rows, cols))
    edge = lane_iota((rows, cols)) >= cols - BORDER
    weights = [jnp.zeros((rows, cols), jnp.float32) for r in range(rank)]
    for c in range(channels):
        dual_ref[c] = factor * shifted_ref[c]
        strip = right_ref[8 * c : 8 * (c + 1)] + corner_ref[8 * c : 8 * (c + 1)]
        strip = unpack_rows(strip, cols - BORDER, groups)
        prior = below_ref[BORDER * c : BORDER * (c + 1)] + jnp.where(edge, strip, 0.0)
        for r in range(rank):
            weights[r] = weights[r] + basis_ref[r, c : c + 1, :] * prior
    for r in range(rank):
        weights[r] = (plain_ref[r] - factor * scaled_ref[r]) - (PRIMAL_STEP * WEIGHT * BAND_STEP) * weights[r]
    for c in range(channels):
        total = basis_ref[0, c : c + 1, :] * weights[0]
        for r in range(1, rank):
            total = total + basis_ref[r, c : c + 1, :] * weights[r]
        image_ref[c] = jnp.maximum(total, 0.0)


def shift(axis_sizes, steps):
    return [
        (
            a * axis_sizes[1] + b,
            (a + steps[0]) % axis_sizes[0] * axis_sizes[1] + (b + steps[1]) % axis_sizes[1],
        )
        for a in range(axis_sizes[0])
        for b in range(axis_sizes[1])
    ]


def add_kernel(value_ref, arrived_ref, *refs):
    refs[-1][...] = value_ref[:8] + arrived_ref[:8]


def doubling():
    rounds = []
    for axis in ("fy", "fx"):
        step = lax.axis_size(axis) // 2
        while step > 1:
            rounds.append((axis, step))
            step //= 2
    return rounds


def partner(value, round_):
    axis, step = round_
    return lax.ppermute(value, axis, [(i, i ^ step) for i in range(lax.axis_size(axis))])


def stamp_kernel(value_ref, arrived_ref, above_in, left_in, corner_in, total_ref, above_ref, left_ref, corner_ref):
    total = value_ref[...] + arrived_ref[...]
    total_ref[...] = total
    for ref in (above_ref, left_ref, corner_ref):
        ref[pl.ds(ref.shape[0] - 8, 8)] = total


def added(value, arrived, *after):
    return pl.pallas_call(
        add_kernel,
        out_shape=jax.ShapeDtypeStruct((8, value.shape[1]), value.dtype),
        in_specs=[pl.BlockSpec(memory_space=pltpu.VMEM)] * 2 + [pl.BlockSpec(memory_space=pl.ANY)] * len(after),
        out_specs=pl.BlockSpec(memory_space=pltpu.VMEM),
        compiler_params=pltpu.CompilerParams(vmem_limit_bytes=1024 * 1024),
        name="add",
    )(value, arrived, *after)


def per_device(start_image, dirty, sampling, basis_seed, margin):
    channels, rows, cols = start_image.shape
    rank = basis_seed.shape[1]
    sizes = (lax.axis_size("fy"), lax.axis_size("fx"))
    half = 2 * rows
    tall = rows + BORDER
    wide = cols + LANES
    radius = BALL_SCALE * math.sqrt(channels * rows * cols * sizes[0] * sizes[1])
    f32, bf16 = jnp.float32, jnp.bfloat16
    image_shape = jax.ShapeDtypeStruct((channels, rows, cols), f32)
    pack_shape = jax.ShapeDtypeStruct((channels, 8, LANES), f32)
    params = pltpu.CompilerParams(vmem_limit_bytes=16 * 1024 * 1024)
    vmem = pl.BlockSpec(memory_space=pltpu.VMEM)
    smem = pl.BlockSpec(memory_space=pltpu.SMEM)
    hbm = pl.BlockSpec(memory_space=pltpu.HBM)
    anywhere = pl.BlockSpec(memory_space=pl.ANY)

    def kept(value):
        return pltpu.with_memory_space_constraint(value, pltpu.HBM)

    def moved(value, steps):
        return lax.ppermute(value, ("fy", "fx"), shift(sizes, steps))

    above = moved(start_image, (1, 0))
    energy, pack, own, gain, shifted = pl.pallas_call(
        first_kernel,
        out_shape=(jax.ShapeDtypeStruct((8, cols), f32), pack_shape, image_shape, image_shape, image_shape),
        in_specs=[hbm] * 3,
        out_specs=(vmem,) * 5,
        scratch_shapes=[pltpu.VMEM((channels, rows, cols), f32), pltpu.SemaphoreType.DMA((1, 3))],
        compiler_params=params,
        name="first",
    )(kept(start_image), kept(dirty), kept(sampling))
    left = moved(pack, (0, 1))
    corner = moved(pack, (1, 1))

    rounds = doubling()
    energy = added(energy, partner(energy, rounds[0]))

    table = row_table(rows)
    table_t = np.ascontiguousarray(table.reshape(LEVELS, half, tall).transpose(0, 2, 1))
    basis, a, a_t, g = pl.pallas_call(
        prepare_kernel,
        out_shape=(
            jax.ShapeDtypeStruct((rank, channels, LANES), f32),
            jax.ShapeDtypeStruct((LEVELS * half, 3 * tall), bf16),
            jax.ShapeDtypeStruct((tall, 3 * LEVELS * half), bf16),
            jax.ShapeDtypeStruct((LEVELS, 2, wide, 2 * cols), bf16),
        ),
        in_specs=[smem, vmem, anywhere, vmem, vmem, vmem],
        out_specs=(vmem,) * 4,
        compiler_params=params,
        cost_estimate=AHEAD,
        name="prepare",
    )(margin, basis_seed.T, energy, table, table_t, col_table(cols))
    for round_ in rounds[1:-1]:
        energy = added(energy, partner(energy, round_), basis)
    arriving = partner(energy, rounds[-1])
    bank_shape = jax.ShapeDtypeStruct((LEVELS, channels, half, wide), bf16)
    z_high, z_low = pl.pallas_call(
        rows_kernel,
        out_shape=(bank_shape, bank_shape),
        in_specs=[vmem] * 5 + [anywhere],
        out_specs=(vmem,) * 2,
        compiler_params=params,
        name="rows",
    )(own, above, left, corner, a, energy)

    above_shape = jax.ShapeDtypeStruct((channels * BORDER + 8, cols), f32)
    strip_shape = jax.ShapeDtypeStruct((channels * 8 + 8, LANES), f32)
    own_part, *parts = pl.pallas_call(
        bank_kernel,
        out_shape=(image_shape, above_shape, strip_shape, strip_shape),
        in_specs=[vmem] * 4,
        out_specs=(vmem,) * 4,
        scratch_shapes=[pltpu.VMEM(bank_shape.shape, bf16)] * 2,
        compiler_params=params,
        name="bank",
    )(z_high, z_low, a_t, g)
    energy, *parts = pl.pallas_call(
        stamp_kernel,
        out_shape=(jax.ShapeDtypeStruct(energy.shape, f32), above_shape, strip_shape, strip_shape),
        in_specs=[vmem] * 5,
        out_specs=(vmem,) * 4,
        input_output_aliases={2: 1, 3: 2, 4: 3},
        compiler_params=pltpu.CompilerParams(vmem_limit_bytes=1024 * 1024),
        name="stamp",
    )(energy, arriving, *parts)
    below = moved(parts[0], (-1, 0))
    right = moved(parts[1], (0, -1))
    corner_back = moved(parts[2], (-1, -1))

    weight_shape = jax.ShapeDtypeStruct((rank, rows, cols), f32)
    plain, scaled = pl.pallas_call(
        begin_kernel,
        out_shape=(weight_shape, weight_shape),
        in_specs=[vmem] * 5 + [anywhere],
        out_specs=(vmem,) * 2,
        compiler_params=params,
        name="begin",
    )(own, shifted, gain, basis, own_part, energy)

    def last(*refs):
        last_kernel(radius, *refs)

    return pl.pallas_call(
        last,
        out_shape=(image_shape, image_shape),
        in_specs=[vmem] * 8,
        compiler_params=params,
        name="last",
    )(shifted, basis, energy, plain, scaled, below, right, corner_back)


def solution(mesh):
    return jax.shard_map(
        per_device,
        mesh=mesh,
        in_specs=(
            P(None, "fy", "fx"),
            P(None, "fy", "fx"),
            P(None, "fy", "fx"),
            P(),
            P("fy", "fx", None, None),
        ),
        out_specs=(P(None, "fy", "fx"), P(None, "fy", "fx")),
        check_vma=False,
    )
```

```python
import math

import jax
import jax.numpy as jnp
import numpy as np
from jax import lax
from jax.experimental import pallas as pl
from jax.experimental.pallas import tpu as pltpu
from jax.sharding import PartitionSpec as P

LEVELS = 2
BORDER = 32
LANES = 128


DAUBECHIES = [
    -0.00011747678400228192,
    0.0006754494059985568,
    -0.0003917403729959771,
    -0.00487035299301066,
    0.008746094047015655,
    0.013981027917015516,
    -0.04408825393106472,
    -0.01736930100202211,
    0.128747426620186,
    0.00047248457399797254,
    -0.2840155429624281,
    -0.015829105256023893,
    0.5853546836548691,
    0.6756307362980128,
    0.3128715909144659,
    0.05441584224308161,
]
DUAL_STEP = 0.5
PRIMAL_STEP = 0.5
CLIP_LEVEL = 0.08
BALL_SCALE = 0.8
NORM_EPS = 1e-06
AHEAD = pl.CostEstimate(flops=10**9, transcendentals=0, bytes_accessed=10**8)
WEIGHT = 1.0 / math.sqrt(LEVELS)
BAND_STEP = DUAL_STEP * WEIGHT

LOW = [tap / math.sqrt(2.0) for tap in DAUBECHIES]
HIGH = [(-1.0) ** k * LOW[len(LOW) - 1 - k] for k in range(len(LOW))]


def band(taps, extent, dilation):
    matrix = np.zeros((BORDER + extent, extent), np.float32)
    for k, tap in enumerate(taps):
        for i in range(extent):
            matrix[i - k * dilation + BORDER, i] += np.float32(tap)
    return matrix


def row_table(rows):
    return np.concatenate(
        [band(taps, rows, 2**level).T for level in range(LEVELS) for taps in (LOW, HIGH)], axis=0
    )


def col_table(cols):
    table = np.zeros((LEVELS, cols + LANES, 2 * cols), np.float32)
    for level in range(LEVELS):
        for half, taps in enumerate((LOW, HIGH)):
            matrix = band(taps, cols, 2**level)
            table[level, :cols, half * cols : (half + 1) * cols] = matrix[BORDER:]
            table[level, cols : cols + BORDER, half * cols : (half + 1) * cols] = matrix[:BORDER]
    return table


def terms(value):
    high = value.astype(jnp.bfloat16)
    low = (value - high.astype(jnp.float32)).astype(jnp.bfloat16)
    return high, low


def dot(a, b):
    return lax.dot_general(a, b, (((1,), (0,)), ((), ())), preferred_element_type=jnp.float32)


def lane_iota(shape):
    return lax.broadcasted_iota(jnp.int32, shape, len(shape) - 1)


def row_iota(shape):
    return lax.broadcasted_iota(jnp.int32, shape, len(shape) - 2)


def pack_rows(strip, offset):
    groups = strip.shape[0] // 8
    lane = lane_iota((8, LANES))
    packed = None
    for q in range(groups):
        piece = strip[8 * q : 8 * q + 8]
        shift = (BORDER * q - offset) % LANES
        if shift:
            piece = pltpu.roll(piece, shift, 1)
        packed = piece if packed is None else jnp.where(lane >= BORDER * q, piece, packed)
    return packed


def unpack_rows(packed, offset, groups):
    pieces = []
    for q in range(groups):
        shift = (offset - BORDER * q) % LANES
        pieces.append(pltpu.roll(packed, shift, 1) if shift else packed)
    return jnp.concatenate(pieces, axis=0)


def first_kernel(
    start_hbm, dirty_hbm, sampling_hbm, energy_ref, pack_ref, own_ref, gain_ref, shifted_ref, dirty_ref, sems
):
    channels, rows, cols = own_ref.shape
    parts = sems.shape[0]
    size = channels // parts
    copies = []
    for part in range(parts):
        at = pl.ds(part * size, size)
        trio = [
            pltpu.make_async_copy(source.at[at], target.at[at], sems.at[part, k])
            for k, (source, target) in enumerate(
                ((start_hbm, own_ref), (sampling_hbm, gain_ref), (dirty_hbm, dirty_ref))
            )
        ]
        for copy in trio:
            copy.start()
        copies.append(trio)
    total = jnp.zeros((8, cols), jnp.float32)
    for part in range(parts):
        for copy in copies[part]:
            copy.wait()
        for c in range(part * size, (part + 1) * size):
            field = own_ref[c]
            shifted = DUAL_STEP * gain_ref[c] * field - DUAL_STEP * dirty_ref[c]
            shifted_ref[c] = shifted
            square = shifted * shifted
            for q in range(rows // 8):
                total = total + square[8 * q : 8 * q + 8]
            pack_ref[c] = pack_rows(field, cols - BORDER)
    energy_ref[:8] = total


def prepare_kernel(
    margin_ref, seed_ref, after_ref, rows_ref, rows_t_ref, cols_ref,
    basis_ref, a_ref, at_ref, g_ref,
):
    rank, channels = seed_ref.shape
    eye = row_iota((channels, channels)) == lane_iota((channels, channels))
    columns = []
    for r in range(rank):
        row = jnp.broadcast_to(seed_ref[r : r + 1, :], (channels, channels))
        column = jnp.sum(jnp.where(eye, row, 0.0), axis=1, keepdims=True)
        columns.append(jnp.broadcast_to(column, (channels, LANES)))
    for r in range(rank):
        vector = columns[r]
        vector = vector / jnp.sqrt(jnp.sum(vector * vector, axis=0, keepdims=True))
        basis_ref[r] = vector
        for later in range(r + 1, rank):
            along = jnp.sum(vector * columns[later], axis=0, keepdims=True)
            columns[later] = columns[later] - along * vector

    half, tall = rows_ref.shape[0] // LEVELS, rows_ref.shape[1]
    wide, double = cols_ref.shape[1:]
    cols = double // 2
    first_row = lax.axis_index("fy") == 0
    first_col = lax.axis_index("fx") == 0
    position = lane_iota((half, tall)) - BORDER
    position_t = row_iota((tall, half)) - BORDER
    a_parts, at_parts = [], []
    for level in range(LEVELS):
        width = jnp.where(first_row, 0, margin_ref[0, 0, level, 0])
        a_parts.append(jnp.where(position >= -width, rows_ref[level * half : (level + 1) * half], 0.0))
        at_parts.append(jnp.where(position_t >= -width, rows_t_ref[level], 0.0))
    a_high, a_low = terms(jnp.concatenate(a_parts, axis=0))
    a_ref[...] = jnp.concatenate([a_high, a_high, a_low], axis=1)
    at_pairs = [terms(part) for part in at_parts]
    at_ref[...] = jnp.concatenate(
        [pair[0] for pair in at_pairs] * 2 + [pair[1] for pair in at_pairs], axis=1
    )
    at = row_iota((wide, double))
    for level in range(LEVELS):
        width = jnp.where(first_col, 0, margin_ref[0, 0, level, 1])
        g = jnp.where((at < cols) | (at >= cols + BORDER - width), cols_ref[level], 0.0)
        g_high, g_low = terms(g)
        g_ref[level, 0] = g_high
        g_ref[level, 1] = g_low


def dot_t(a, b):
    return lax.dot_general(a, b, (((1,), (1,)), ((), ())), preferred_element_type=jnp.float32)


def bank_kernel(
    own_ref, above_ref, corner_ref, left_ref, a_ref, at_ref, g_ref, after_ref,
    own_out, above_out, left_out, corner_out, z_high, z_low, u_high, u_low,
):
    channels, rows, cols = own_out.shape
    wide = cols + LANES
    half = 2 * rows
    size = channels // 4
    groups = rows // 8

    for c in range(channels):
        upper = jnp.concatenate([above_ref[c], unpack_rows(corner_ref[c], 0, groups)], axis=1)
        lower = jnp.concatenate([own_ref[c], unpack_rows(left_ref[c], 0, groups)], axis=1)
        e_high, e_low = terms(jnp.concatenate([upper, lower], axis=0))
        z = dot(a_ref[...], jnp.concatenate([e_high, e_low, e_high], axis=0))
        part_high, part_low = terms(z)
        for level in range(LEVELS):
            z_high[level, c] = part_high[level * half : (level + 1) * half]
            z_low[level, c] = part_low[level * half : (level + 1) * half]

    low_rows = row_iota((half, 2 * cols)) < rows
    low_cols = lane_iota((half, 2 * cols)) < cols
    bound = jnp.where(low_rows & low_cols, 0.0, CLIP_LEVEL / BAND_STEP)
    for level in range(LEVELS):
        g_high, g_low = g_ref[level, 0], g_ref[level, 1]
        for start in range(0, channels, size):
            span = slice(start, start + size)
            zh = z_high[level, span].reshape(size * half, wide)
            zl = z_low[level, span].reshape(size * half, wide)
            coef = dot(jnp.concatenate([zh, zl, zh], axis=1), jnp.concatenate([g_high, g_high, g_low], axis=0))
            coef = coef.reshape(size, half, 2 * cols)
            coef = jnp.minimum(jnp.maximum(coef, -bound), bound).reshape(size * half, 2 * cols)
            t_high, t_low = terms(coef)
            u = dot_t(
                jnp.concatenate([t_high, t_low, t_high], axis=1),
                jnp.concatenate([g_high, g_high, g_low], axis=1),
            )
            part_high, part_low = terms(u)
            u_high[level, span] = part_high.reshape(size, half, wide)
            u_low[level, span] = part_low.reshape(size, half, wide)

    for c in range(channels):
        highs = [u_high[level, c] for level in range(LEVELS)]
        lows = [u_low[level, c] for level in range(LEVELS)]
        back = dot(at_ref[...], jnp.concatenate(highs + lows + highs, axis=0))
        above_out[BORDER * c : BORDER * (c + 1)] = back[:BORDER, :cols]
        own_out[c] = back[BORDER:, :cols]
        corner_out[8 * c : 8 * (c + 1)] = pack_rows(back[:BORDER, cols:], 0)
        left_out[8 * c : 8 * (c + 1)] = pack_rows(back[BORDER:, cols:], 0)


def begin_kernel(own_ref, shifted_ref, gain_ref, basis_ref, part_ref, after_ref, plain_ref, scaled_ref):
    channels, rows, cols = own_ref.shape
    rank = basis_ref.shape[0]
    plain = [jnp.zeros((rows, cols), jnp.float32) for r in range(rank)]
    scaled = [jnp.zeros((rows, cols), jnp.float32) for r in range(rank)]
    for c in range(channels):
        first = own_ref[c] - (PRIMAL_STEP * WEIGHT * BAND_STEP) * part_ref[c]
        second = PRIMAL_STEP * gain_ref[c] * shifted_ref[c]
        for r in range(rank):
            plain[r] = plain[r] + basis_ref[r, c : c + 1, :] * first
            scaled[r] = scaled[r] + basis_ref[r, c : c + 1, :] * second
    for r in range(rank):
        plain_ref[r] = plain[r]
        scaled_ref[r] = scaled[r]


def last_kernel(
    radius, shifted_ref, basis_ref, energy_ref, plain_ref, scaled_ref, below_ref, right_ref, corner_ref,
    image_ref, dual_ref,
):
    channels, rows, cols = shifted_ref.shape
    rank = basis_ref.shape[0]
    groups = rows // 8
    energy = energy_ref[...]
    for ref in (below_ref, right_ref, corner_ref):
        energy = energy + ref[pl.ds(ref.shape[0] - 8, 8)]
    energy = jnp.sum(jnp.sum(energy, axis=0, keepdims=True), axis=1, keepdims=True)
    factor = jnp.maximum(0.0, 1.0 - DUAL_STEP * radius / jnp.sqrt(energy + NORM_EPS))
    factor = jnp.broadcast_to(factor, (rows, cols))
    edge = lane_iota((rows, cols)) >= cols - BORDER
    weights = [jnp.zeros((rows, cols), jnp.float32) for r in range(rank)]
    for c in range(channels):
        dual_ref[c] = factor * shifted_ref[c]
        strip = right_ref[8 * c : 8 * (c + 1)] + corner_ref[8 * c : 8 * (c + 1)]
        strip = unpack_rows(strip, cols - BORDER, groups)
        prior = below_ref[BORDER * c : BORDER * (c + 1)] + jnp.where(edge, strip, 0.0)
        for r in range(rank):
            weights[r] = weights[r] + basis_ref[r, c : c + 1, :] * prior
    for r in range(rank):
        weights[r] = (plain_ref[r] - factor * scaled_ref[r]) - (PRIMAL_STEP * WEIGHT * BAND_STEP) * weights[r]
    for c in range(channels):
        total = basis_ref[0, c : c + 1, :] * weights[0]
        for r in range(1, rank):
            total = total + basis_ref[r, c : c + 1, :] * weights[r]
        image_ref[c] = jnp.maximum(total, 0.0)


def shift(axis_sizes, steps):
    return [
        (
            a * axis_sizes[1] + b,
            (a + steps[0]) % axis_sizes[0] * axis_sizes[1] + (b + steps[1]) % axis_sizes[1],
        )
        for a in range(axis_sizes[0])
        for b in range(axis_sizes[1])
    ]


def add_kernel(value_ref, arrived_ref, *refs):
    refs[-1][...] = value_ref[:8] + arrived_ref[:8]


def doubling():
    rounds = []
    for axis in ("fy", "fx"):
        step = lax.axis_size(axis) // 2
        while step > 1:
            rounds.append((axis, step))
            step //= 2
    return rounds


def partner(value, round_):
    axis, step = round_
    return lax.ppermute(value, axis, [(i, i ^ step) for i in range(lax.axis_size(axis))])


def stamp_kernel(value_ref, arrived_ref, above_in, left_in, corner_in, total_ref, above_ref, left_ref, corner_ref):
    total = value_ref[...] + arrived_ref[...]
    total_ref[...] = total
    for ref in (above_ref, left_ref, corner_ref):
        ref[pl.ds(ref.shape[0] - 8, 8)] = total


def added(value, arrived, *after):
    return pl.pallas_call(
        add_kernel,
        out_shape=jax.ShapeDtypeStruct((8, value.shape[1]), value.dtype),
        in_specs=[pl.BlockSpec(memory_space=pltpu.VMEM)] * 2 + [pl.BlockSpec(memory_space=pl.ANY)] * len(after),
        out_specs=pl.BlockSpec(memory_space=pltpu.VMEM),
        compiler_params=pltpu.CompilerParams(vmem_limit_bytes=1024 * 1024),
        name="add",
    )(value, arrived, *after)


def per_device(start_image, dirty, sampling, basis_seed, margin):
    channels, rows, cols = start_image.shape
    rank = basis_seed.shape[1]
    sizes = (lax.axis_size("fy"), lax.axis_size("fx"))
    half = 2 * rows
    tall = rows + BORDER
    wide = cols + LANES
    radius = BALL_SCALE * math.sqrt(channels * rows * cols * sizes[0] * sizes[1])
    f32, bf16 = jnp.float32, jnp.bfloat16
    image_shape = jax.ShapeDtypeStruct((channels, rows, cols), f32)
    pack_shape = jax.ShapeDtypeStruct((channels, 8, LANES), f32)
    params = pltpu.CompilerParams(vmem_limit_bytes=16 * 1024 * 1024)
    vmem = pl.BlockSpec(memory_space=pltpu.VMEM)
    smem = pl.BlockSpec(memory_space=pltpu.SMEM)
    hbm = pl.BlockSpec(memory_space=pltpu.HBM)
    anywhere = pl.BlockSpec(memory_space=pl.ANY)

    def kept(value):
        return pltpu.with_memory_space_constraint(value, pltpu.HBM)

    def moved(value, steps):
        return lax.ppermute(value, ("fy", "fx"), shift(sizes, steps))

    above = moved(start_image, (1, 0))
    energy, pack, own, gain, shifted = pl.pallas_call(
        first_kernel,
        out_shape=(jax.ShapeDtypeStruct((8, cols), f32), pack_shape, image_shape, image_shape, image_shape),
        in_specs=[hbm] * 3,
        out_specs=(vmem,) * 5,
        scratch_shapes=[pltpu.VMEM((channels, rows, cols), f32), pltpu.SemaphoreType.DMA((1, 3))],
        compiler_params=params,
        name="first",
    )(kept(start_image), kept(dirty), kept(sampling))
    left = moved(pack, (0, 1))
    corner = moved(pack, (1, 1))

    rounds = doubling()
    energy = added(energy, partner(energy, rounds[0]))

    table = row_table(rows)
    table_t = np.ascontiguousarray(table.reshape(LEVELS, half, tall).transpose(0, 2, 1))
    basis, a, a_t, g = pl.pallas_call(
        prepare_kernel,
        out_shape=(
            jax.ShapeDtypeStruct((rank, channels, LANES), f32),
            jax.ShapeDtypeStruct((LEVELS * half, 3 * tall), bf16),
            jax.ShapeDtypeStruct((tall, 3 * LEVELS * half), bf16),
            jax.ShapeDtypeStruct((LEVELS, 2, wide, 2 * cols), bf16),
        ),
        in_specs=[smem, vmem, anywhere, vmem, vmem, vmem],
        out_specs=(vmem,) * 4,
        compiler_params=params,
        cost_estimate=AHEAD,
        name="prepare",
    )(margin, basis_seed.T, energy, table, table_t, col_table(cols))
    for round_ in rounds[1:-1]:
        energy = added(energy, partner(energy, round_), basis)
    arriving = partner(energy, rounds[-1])
    above_shape = jax.ShapeDtypeStruct((channels * BORDER + 8, cols), f32)
    strip_shape = jax.ShapeDtypeStruct((channels * 8 + 8, LANES), f32)
    own_part, *parts = pl.pallas_call(
        bank_kernel,
        out_shape=(image_shape, above_shape, strip_shape, strip_shape),
        in_specs=[vmem] * 7 + [anywhere],
        out_specs=(vmem,) * 4,
        scratch_shapes=[pltpu.VMEM((LEVELS, channels, half, wide), bf16)] * 4,
        compiler_params=params,
        name="bank",
    )(own, above, corner, left, a, a_t, g, energy)
    energy, *parts = pl.pallas_call(
        stamp_kernel,
        out_shape=(jax.ShapeDtypeStruct(energy.shape, f32), above_shape, strip_shape, strip_shape),
        in_specs=[vmem] * 5,
        out_specs=(vmem,) * 4,
        input_output_aliases={2: 1, 3: 2, 4: 3},
        compiler_params=pltpu.CompilerParams(vmem_limit_bytes=1024 * 1024),
        name="stamp",
    )(energy, arriving, *parts)
    below = moved(parts[0], (-1, 0))
    right = moved(parts[1], (0, -1))
    corner_back = moved(parts[2], (-1, -1))

    weight_shape = jax.ShapeDtypeStruct((rank, rows, cols), f32)
    plain, scaled = pl.pallas_call(
        begin_kernel,
        out_shape=(weight_shape, weight_shape),
        in_specs=[vmem] * 5 + [anywhere],
        out_specs=(vmem,) * 2,
        compiler_params=params,
        name="begin",
    )(own, shifted, gain, basis, own_part, energy)

    def last(*refs):
        last_kernel(radius, *refs)

    return pl.pallas_call(
        last,
        out_shape=(image_shape, image_shape),
        in_specs=[vmem] * 8,
        compiler_params=params,
        name="last",
    )(shifted, basis, energy, plain, scaled, below, right, corner_back)


def solution(mesh):
    return jax.shard_map(
        per_device,
        mesh=mesh,
        in_specs=(
            P(None, "fy", "fx"),
            P(None, "fy", "fx"),
            P(None, "fy", "fx"),
            P(),
            P("fy", "fx", None, None),
        ),
        out_specs=(P(None, "fy", "fx"), P(None, "fy", "fx")),
        check_vma=False,
    )
```

```python
import math

import jax
import jax.numpy as jnp
import numpy as np
from jax import lax
from jax.experimental import pallas as pl
from jax.experimental.pallas import tpu as pltpu
from jax.sharding import PartitionSpec as P

LEVELS = 2
BORDER = 32
LANES = 128


DAUBECHIES = [
    -0.00011747678400228192,
    0.0006754494059985568,
    -0.0003917403729959771,
    -0.00487035299301066,
    0.008746094047015655,
    0.013981027917015516,
    -0.04408825393106472,
    -0.01736930100202211,
    0.128747426620186,
    0.00047248457399797254,
    -0.2840155429624281,
    -0.015829105256023893,
    0.5853546836548691,
    0.6756307362980128,
    0.3128715909144659,
    0.05441584224308161,
]
DUAL_STEP = 0.5
PRIMAL_STEP = 0.5
CLIP_LEVEL = 0.08
BALL_SCALE = 0.8
NORM_EPS = 1e-06
AHEAD = pl.CostEstimate(flops=10**9, transcendentals=0, bytes_accessed=10**8)
WEIGHT = 1.0 / math.sqrt(LEVELS)
BAND_STEP = DUAL_STEP * WEIGHT

LOW = [tap / math.sqrt(2.0) for tap in DAUBECHIES]
HIGH = [(-1.0) ** k * LOW[len(LOW) - 1 - k] for k in range(len(LOW))]


def band(taps, extent, dilation):
    matrix = np.zeros((BORDER + extent, extent), np.float32)
    for k, tap in enumerate(taps):
        for i in range(extent):
            matrix[i - k * dilation + BORDER, i] += np.float32(tap)
    return matrix


def row_table(rows):
    return np.concatenate(
        [band(taps, rows, 2**level).T for level in range(LEVELS) for taps in (LOW, HIGH)], axis=0
    )


def col_table(cols):
    table = np.zeros((LEVELS, cols + LANES, 2 * cols), np.float32)
    for level in range(LEVELS):
        for half, taps in enumerate((LOW, HIGH)):
            matrix = band(taps, cols, 2**level)
            table[level, :cols, half * cols : (half + 1) * cols] = matrix[BORDER:]
            table[level, cols : cols + BORDER, half * cols : (half + 1) * cols] = matrix[:BORDER]
    return table


def terms(value):
    high = value.astype(jnp.bfloat16)
    low = (value - high.astype(jnp.float32)).astype(jnp.bfloat16)
    return high, low


def dot(a, b):
    return lax.dot_general(a, b, (((1,), (0,)), ((), ())), preferred_element_type=jnp.float32)


def lane_iota(shape):
    return lax.broadcasted_iota(jnp.int32, shape, len(shape) - 1)


def row_iota(shape):
    return lax.broadcasted_iota(jnp.int32, shape, len(shape) - 2)


def pack_rows(strip, offset):
    groups = strip.shape[0] // 8
    lane = lane_iota((8, LANES))
    packed = None
    for q in range(groups):
        piece = strip[8 * q : 8 * q + 8]
        shift = (BORDER * q - offset) % LANES
        if shift:
            piece = pltpu.roll(piece, shift, 1)
        packed = piece if packed is None else jnp.where(lane >= BORDER * q, piece, packed)
    return packed


def unpack_rows(packed, offset, groups):
    pieces = []
    for q in range(groups):
        shift = (offset - BORDER * q) % LANES
        pieces.append(pltpu.roll(packed, shift, 1) if shift else packed)
    return jnp.concatenate(pieces, axis=0)


def first_kernel(
    start_hbm, dirty_hbm, sampling_hbm, energy_ref, pack_ref, own_ref, gain_ref, shifted_ref, dirty_ref, sems
):
    channels, rows, cols = own_ref.shape
    parts = sems.shape[0]
    size = channels // parts
    copies = []
    for part in range(parts):
        at = pl.ds(part * size, size)
        trio = [
            pltpu.make_async_copy(source.at[at], target.at[at], sems.at[part, k])
            for k, (source, target) in enumerate(
                ((start_hbm, own_ref), (sampling_hbm, gain_ref), (dirty_hbm, dirty_ref))
            )
        ]
        for copy in trio:
            copy.start()
        copies.append(trio)
    total = jnp.zeros((8, cols), jnp.float32)
    for part in range(parts):
        for copy in copies[part]:
            copy.wait()
        for c in range(part * size, (part + 1) * size):
            field = own_ref[c]
            shifted = DUAL_STEP * gain_ref[c] * field - DUAL_STEP * dirty_ref[c]
            shifted_ref[c] = shifted
            square = shifted * shifted
            for q in range(rows // 8):
                total = total + square[8 * q : 8 * q + 8]
            pack_ref[c] = pack_rows(field, cols - BORDER)
    energy_ref[:8] = total


def prepare_kernel(
    margin_ref, seed_ref, after_ref, rows_ref, rows_t_ref, cols_ref,
    basis_ref, a_ref, at_ref, g_ref,
):
    rank, channels = seed_ref.shape
    eye = row_iota((channels, channels)) == lane_iota((channels, channels))
    columns = []
    for r in range(rank):
        row = jnp.broadcast_to(seed_ref[r : r + 1, :], (channels, channels))
        column = jnp.sum(jnp.where(eye, row, 0.0), axis=1, keepdims=True)
        columns.append(jnp.broadcast_to(column, (channels, LANES)))
    for r in range(rank):
        vector = columns[r]
        vector = vector / jnp.sqrt(jnp.sum(vector * vector, axis=0, keepdims=True))
        basis_ref[r] = vector
        for later in range(r + 1, rank):
            along = jnp.sum(vector * columns[later], axis=0, keepdims=True)
            columns[later] = columns[later] - along * vector

    half, tall = rows_ref.shape[0] // LEVELS, rows_ref.shape[1]
    wide, double = cols_ref.shape[1:]
    cols = double // 2
    first_row = lax.axis_index("fy") == 0
    first_col = lax.axis_index("fx") == 0
    position = lane_iota((half, tall)) - BORDER
    position_t = row_iota((tall, half)) - BORDER
    a_parts, at_parts = [], []
    for level in range(LEVELS):
        width = jnp.where(first_row, 0, margin_ref[0, 0, level, 0])
        a_parts.append(jnp.where(position >= -width, rows_ref[level * half : (level + 1) * half], 0.0))
        at_parts.append(jnp.where(position_t >= -width, rows_t_ref[level], 0.0))
    a_high, a_low = terms(jnp.concatenate(a_parts, axis=0))
    a_ref[...] = jnp.concatenate([a_high, a_high, a_low], axis=1)
    at_pairs = [terms(part) for part in at_parts]
    at_ref[...] = jnp.concatenate(
        [pair[0] for pair in at_pairs] * 2 + [pair[1] for pair in at_pairs], axis=1
    )
    at = row_iota((wide, double))
    for level in range(LEVELS):
        width = jnp.where(first_col, 0, margin_ref[0, 0, level, 1])
        g = jnp.where((at < cols) | (at >= cols + BORDER - width), cols_ref[level], 0.0)
        g_high, g_low = terms(g)
        g_ref[level, 0] = g_high
        g_ref[level, 1] = g_low


def dot_t(a, b):
    return lax.dot_general(a, b, (((1,), (1,)), ((), ())), preferred_element_type=jnp.float32)


def bank_kernel(
    own_ref, above_ref, corner_ref, left_ref, a_ref, at_ref, g_ref, after_ref,
    own_out, above_out, left_out, corner_out, z_high, z_low, u_high, u_low,
):
    channels, rows, cols = own_out.shape
    wide = cols + LANES
    half = 2 * rows
    size = channels // 4
    groups = rows // 8

    for c in range(channels):
        upper = jnp.concatenate([above_ref[c], unpack_rows(corner_ref[c], 0, groups)], axis=1)
        lower = jnp.concatenate([own_ref[c], unpack_rows(left_ref[c], 0, groups)], axis=1)
        e_high, e_low = terms(jnp.concatenate([upper, lower], axis=0))
        z = dot(a_ref[...], jnp.concatenate([e_high, e_low, e_high], axis=0))
        part_high, part_low = terms(z)
        for level in range(LEVELS):
            z_high[level, c] = part_high[level * half : (level + 1) * half]
            z_low[level, c] = part_low[level * half : (level + 1) * half]

    low_rows = row_iota((half, 2 * cols)) < rows
    low_cols = lane_iota((half, 2 * cols)) < cols
    bound = jnp.where(low_rows & low_cols, 0.0, CLIP_LEVEL / BAND_STEP)
    for level in range(LEVELS):
        g_high, g_low = g_ref[level, 0], g_ref[level, 1]
        for start in range(0, channels, size):
            span = slice(start, start + size)
            zh = z_high[level, span].reshape(size * half, wide)
            zl = z_low[level, span].reshape(size * half, wide)
            coef = dot(jnp.concatenate([zh, zl, zh], axis=1), jnp.concatenate([g_high, g_high, g_low], axis=0))
            coef = coef.reshape(size, half, 2 * cols)
            coef = jnp.minimum(jnp.maximum(coef, -bound), bound).reshape(size * half, 2 * cols)
            t_high, t_low = terms(coef)
            u = dot_t(
                jnp.concatenate([t_high, t_low, t_high], axis=1),
                jnp.concatenate([g_high, g_high, g_low], axis=1),
            )
            part_high, part_low = terms(u)
            u_high[level, span] = part_high.reshape(size, half, wide)
            u_low[level, span] = part_low.reshape(size, half, wide)

    for c in range(channels):
        highs = [u_high[level, c] for level in range(LEVELS)]
        lows = [u_low[level, c] for level in range(LEVELS)]
        back = dot(at_ref[...], jnp.concatenate(highs + lows + highs, axis=0))
        above_out[BORDER * c : BORDER * (c + 1)] = back[:BORDER, :cols]
        own_out[c] = back[BORDER:, :cols]
        corner_out[8 * c : 8 * (c + 1)] = pack_rows(back[:BORDER, cols:], 0)
        left_out[8 * c : 8 * (c + 1)] = pack_rows(back[BORDER:, cols:], 0)


def begin_kernel(own_ref, shifted_ref, gain_ref, basis_ref, part_ref, after_ref, plain_ref, scaled_ref):
    channels, rows, cols = own_ref.shape
    rank = basis_ref.shape[0]
    plain = [jnp.zeros((rows, cols), jnp.float32) for r in range(rank)]
    scaled = [jnp.zeros((rows, cols), jnp.float32) for r in range(rank)]
    for c in range(channels):
        first = own_ref[c] - (PRIMAL_STEP * WEIGHT * BAND_STEP) * part_ref[c]
        second = PRIMAL_STEP * gain_ref[c] * shifted_ref[c]
        for r in range(rank):
            plain[r] = plain[r] + basis_ref[r, c : c + 1, :] * first
            scaled[r] = scaled[r] + basis_ref[r, c : c + 1, :] * second
    for r in range(rank):
        plain_ref[r] = plain[r]
        scaled_ref[r] = scaled[r]


def last_kernel(
    radius, shifted_ref, basis_ref, energy_ref, plain_ref, scaled_ref, below_ref, right_ref, corner_ref,
    image_hbm, dual_hbm, image_ref, dual_ref, sems,
):
    channels, rows, cols = shifted_ref.shape
    parts = sems.shape[1]
    size = channels // parts
    copies = []

    def send(k, part):
        at = pl.ds(part * size, size)
        source, target = ((dual_ref, dual_hbm), (image_ref, image_hbm))[k]
        copies.append(pltpu.make_async_copy(source.at[at], target.at[at], sems.at[k, part]))
        copies[-1].start()

    rank = basis_ref.shape[0]
    groups = rows // 8
    energy = energy_ref[...]
    for ref in (below_ref, right_ref, corner_ref):
        energy = energy + ref[pl.ds(ref.shape[0] - 8, 8)]
    energy = jnp.sum(jnp.sum(energy, axis=0, keepdims=True), axis=1, keepdims=True)
    factor = jnp.maximum(0.0, 1.0 - DUAL_STEP * radius / jnp.sqrt(energy + NORM_EPS))
    factor = jnp.broadcast_to(factor, (rows, cols))
    edge = lane_iota((rows, cols)) >= cols - BORDER
    weights = [jnp.zeros((rows, cols), jnp.float32) for r in range(rank)]
    for c in range(channels):
        dual_ref[c] = factor * shifted_ref[c]
        if (c + 1) % size == 0:
            send(0, c // size)
    for c in range(channels):
        strip = right_ref[8 * c : 8 * (c + 1)] + corner_ref[8 * c : 8 * (c + 1)]
        strip = unpack_rows(strip, cols - BORDER, groups)
        prior = below_ref[BORDER * c : BORDER * (c + 1)] + jnp.where(edge, strip, 0.0)
        for r in range(rank):
            weights[r] = weights[r] + basis_ref[r, c : c + 1, :] * prior
    for r in range(rank):
        weights[r] = (plain_ref[r] - factor * scaled_ref[r]) - (PRIMAL_STEP * WEIGHT * BAND_STEP) * weights[r]
    for c in range(channels):
        total = basis_ref[0, c : c + 1, :] * weights[0]
        for r in range(1, rank):
            total = total + basis_ref[r, c : c + 1, :] * weights[r]
        image_ref[c] = jnp.maximum(total, 0.0)
        if (c + 1) % size == 0:
            send(1, c // size)
    for copy in copies:
        copy.wait()


def shift(axis_sizes, steps):
    return [
        (
            a * axis_sizes[1] + b,
            (a + steps[0]) % axis_sizes[0] * axis_sizes[1] + (b + steps[1]) % axis_sizes[1],
        )
        for a in range(axis_sizes[0])
        for b in range(axis_sizes[1])
    ]


def add_kernel(value_ref, arrived_ref, *refs):
    refs[-1][...] = value_ref[:8] + arrived_ref[:8]


def doubling():
    rounds = []
    for axis in ("fy", "fx"):
        step = lax.axis_size(axis) // 2
        while step > 1:
            rounds.append((axis, step))
            step //= 2
    return rounds


def partner(value, round_):
    axis, step = round_
    return lax.ppermute(value, axis, [(i, i ^ step) for i in range(lax.axis_size(axis))])


def stamp_kernel(value_ref, arrived_ref, above_in, left_in, corner_in, total_ref, above_ref, left_ref, corner_ref):
    total = value_ref[...] + arrived_ref[...]
    total_ref[...] = total
    for ref in (above_ref, left_ref, corner_ref):
        ref[pl.ds(ref.shape[0] - 8, 8)] = total


def added(value, arrived, *after):
    return pl.pallas_call(
        add_kernel,
        out_shape=jax.ShapeDtypeStruct((8, value.shape[1]), value.dtype),
        in_specs=[pl.BlockSpec(memory_space=pltpu.VMEM)] * 2 + [pl.BlockSpec(memory_space=pl.ANY)] * len(after),
        out_specs=pl.BlockSpec(memory_space=pltpu.VMEM),
        compiler_params=pltpu.CompilerParams(vmem_limit_bytes=1024 * 1024),
        name="add",
    )(value, arrived, *after)


def per_device(start_image, dirty, sampling, basis_seed, margin):
    channels, rows, cols = start_image.shape
    rank = basis_seed.shape[1]
    sizes = (lax.axis_size("fy"), lax.axis_size("fx"))
    half = 2 * rows
    tall = rows + BORDER
    wide = cols + LANES
    radius = BALL_SCALE * math.sqrt(channels * rows * cols * sizes[0] * sizes[1])
    f32, bf16 = jnp.float32, jnp.bfloat16
    image_shape = jax.ShapeDtypeStruct((channels, rows, cols), f32)
    pack_shape = jax.ShapeDtypeStruct((channels, 8, LANES), f32)
    params = pltpu.CompilerParams(vmem_limit_bytes=16 * 1024 * 1024)
    vmem = pl.BlockSpec(memory_space=pltpu.VMEM)
    smem = pl.BlockSpec(memory_space=pltpu.SMEM)
    hbm = pl.BlockSpec(memory_space=pltpu.HBM)
    anywhere = pl.BlockSpec(memory_space=pl.ANY)

    def kept(value):
        return pltpu.with_memory_space_constraint(value, pltpu.HBM)

    def moved(value, steps):
        return lax.ppermute(value, ("fy", "fx"), shift(sizes, steps))

    above = moved(start_image, (1, 0))
    energy, pack, own, gain, shifted = pl.pallas_call(
        first_kernel,
        out_shape=(jax.ShapeDtypeStruct((8, cols), f32), pack_shape, image_shape, image_shape, image_shape),
        in_specs=[hbm] * 3,
        out_specs=(vmem,) * 5,
        scratch_shapes=[pltpu.VMEM((channels, rows, cols), f32), pltpu.SemaphoreType.DMA((1, 3))],
        compiler_params=params,
        name="first",
    )(kept(start_image), kept(dirty), kept(sampling))
    left = moved(pack, (0, 1))
    corner = moved(pack, (1, 1))

    rounds = doubling()
    energy = added(energy, partner(energy, rounds[0]))

    table = row_table(rows)
    table_t = np.ascontiguousarray(table.reshape(LEVELS, half, tall).transpose(0, 2, 1))
    basis, a, a_t, g = pl.pallas_call(
        prepare_kernel,
        out_shape=(
            jax.ShapeDtypeStruct((rank, channels, LANES), f32),
            jax.ShapeDtypeStruct((LEVELS * half, 3 * tall), bf16),
            jax.ShapeDtypeStruct((tall, 3 * LEVELS * half), bf16),
            jax.ShapeDtypeStruct((LEVELS, 2, wide, 2 * cols), bf16),
        ),
        in_specs=[smem, vmem, anywhere, vmem, vmem, vmem],
        out_specs=(vmem,) * 4,
        compiler_params=params,
        cost_estimate=AHEAD,
        name="prepare",
    )(margin, basis_seed.T, energy, table, table_t, col_table(cols))
    for round_ in rounds[1:-1]:
        energy = added(energy, partner(energy, round_), basis)
    arriving = partner(energy, rounds[-1])
    above_shape = jax.ShapeDtypeStruct((channels * BORDER + 8, cols), f32)
    strip_shape = jax.ShapeDtypeStruct((channels * 8 + 8, LANES), f32)
    own_part, *parts = pl.pallas_call(
        bank_kernel,
        out_shape=(image_shape, above_shape, strip_shape, strip_shape),
        in_specs=[vmem] * 7 + [anywhere],
        out_specs=(vmem,) * 4,
        scratch_shapes=[pltpu.VMEM((LEVELS, channels, half, wide), bf16)] * 4,
        compiler_params=params,
        name="bank",
    )(own, above, corner, left, a, a_t, g, energy)
    energy, *parts = pl.pallas_call(
        stamp_kernel,
        out_shape=(jax.ShapeDtypeStruct(energy.shape, f32), above_shape, strip_shape, strip_shape),
        in_specs=[vmem] * 5,
        out_specs=(vmem,) * 4,
        input_output_aliases={2: 1, 3: 2, 4: 3},
        compiler_params=pltpu.CompilerParams(vmem_limit_bytes=1024 * 1024),
        name="stamp",
    )(energy, arriving, *parts)
    below = moved(parts[0], (-1, 0))
    right = moved(parts[1], (0, -1))
    corner_back = moved(parts[2], (-1, -1))

    weight_shape = jax.ShapeDtypeStruct((rank, rows, cols), f32)
    plain, scaled = pl.pallas_call(
        begin_kernel,
        out_shape=(weight_shape, weight_shape),
        in_specs=[vmem] * 5 + [anywhere],
        out_specs=(vmem,) * 2,
        compiler_params=params,
        name="begin",
    )(own, shifted, gain, basis, own_part, energy)

    def last(*refs):
        last_kernel(radius, *refs)

    return pl.pallas_call(
        last,
        out_shape=(image_shape, image_shape),
        in_specs=[vmem] * 8,
        out_specs=(hbm, hbm),
        scratch_shapes=[
            pltpu.VMEM(image_shape.shape, f32),
            pltpu.VMEM(image_shape.shape, f32),
            pltpu.SemaphoreType.DMA((2, 2)),
        ],
        compiler_params=params,
        name="last",
    )(shifted, basis, energy, plain, scaled, below, right, corner_back)


def solution(mesh):
    return jax.shard_map(
        per_device,
        mesh=mesh,
        in_specs=(
            P(None, "fy", "fx"),
            P(None, "fy", "fx"),
            P(None, "fy", "fx"),
            P(),
            P("fy", "fx", None, None),
        ),
        out_specs=(P(None, "fy", "fx"), P(None, "fy", "fx")),
        check_vma=False,
    )
```

```python
import math

import jax
import jax.numpy as jnp
import numpy as np
from jax import lax
from jax.experimental import pallas as pl
from jax.experimental.pallas import tpu as pltpu
from jax.sharding import PartitionSpec as P

LEVELS = 2
BORDER = 32
LANES = 128


DAUBECHIES = [
    -0.00011747678400228192,
    0.0006754494059985568,
    -0.0003917403729959771,
    -0.00487035299301066,
    0.008746094047015655,
    0.013981027917015516,
    -0.04408825393106472,
    -0.01736930100202211,
    0.128747426620186,
    0.00047248457399797254,
    -0.2840155429624281,
    -0.015829105256023893,
    0.5853546836548691,
    0.6756307362980128,
    0.3128715909144659,
    0.05441584224308161,
]
DUAL_STEP = 0.5
PRIMAL_STEP = 0.5
CLIP_LEVEL = 0.08
BALL_SCALE = 0.8
NORM_EPS = 1e-06
AHEAD = pl.CostEstimate(flops=10**9, transcendentals=0, bytes_accessed=10**8)
WEIGHT = 1.0 / math.sqrt(LEVELS)
BAND_STEP = DUAL_STEP * WEIGHT

LOW = [tap / math.sqrt(2.0) for tap in DAUBECHIES]
HIGH = [(-1.0) ** k * LOW[len(LOW) - 1 - k] for k in range(len(LOW))]


def band(taps, extent, dilation):
    matrix = np.zeros((BORDER + extent, extent), np.float32)
    for k, tap in enumerate(taps):
        for i in range(extent):
            matrix[i - k * dilation + BORDER, i] += np.float32(tap)
    return matrix


def row_table(rows):
    return np.concatenate(
        [band(taps, rows, 2**level).T for level in range(LEVELS) for taps in (LOW, HIGH)], axis=0
    )


def col_table(cols):
    table = np.zeros((LEVELS, cols + LANES, 2 * cols), np.float32)
    for level in range(LEVELS):
        for half, taps in enumerate((LOW, HIGH)):
            matrix = band(taps, cols, 2**level)
            table[level, :cols, half * cols : (half + 1) * cols] = matrix[BORDER:]
            table[level, cols : cols + BORDER, half * cols : (half + 1) * cols] = matrix[:BORDER]
    return table


def terms(value):
    high = value.astype(jnp.bfloat16)
    low = (value - high.astype(jnp.float32)).astype(jnp.bfloat16)
    return high, low


def dot(a, b):
    return lax.dot_general(a, b, (((1,), (0,)), ((), ())), preferred_element_type=jnp.float32)


def lane_iota(shape):
    return lax.broadcasted_iota(jnp.int32, shape, len(shape) - 1)


def row_iota(shape):
    return lax.broadcasted_iota(jnp.int32, shape, len(shape) - 2)


def pack_rows(strip, offset):
    groups = strip.shape[0] // 8
    lane = lane_iota((8, LANES))
    packed = None
    for q in range(groups):
        piece = strip[8 * q : 8 * q + 8]
        shift = (BORDER * q - offset) % LANES
        if shift:
            piece = pltpu.roll(piece, shift, 1)
        packed = piece if packed is None else jnp.where(lane >= BORDER * q, piece, packed)
    return packed


def unpack_rows(packed, offset, groups):
    pieces = []
    for q in range(groups):
        shift = (offset - BORDER * q) % LANES
        pieces.append(pltpu.roll(packed, shift, 1) if shift else packed)
    return jnp.concatenate(pieces, axis=0)


def first_kernel(
    start_hbm, dirty_hbm, sampling_hbm, energy_ref, pack_ref, own_ref, gain_ref, shifted_ref, dirty_ref, sems
):
    channels, rows, cols = own_ref.shape
    parts = sems.shape[0]
    size = channels // parts
    copies = []
    for part in range(parts):
        at = pl.ds(part * size, size)
        trio = [
            pltpu.make_async_copy(source.at[at], target.at[at], sems.at[part, k])
            for k, (source, target) in enumerate(
                ((start_hbm, own_ref), (sampling_hbm, gain_ref), (dirty_hbm, dirty_ref))
            )
        ]
        for copy in trio:
            copy.start()
        copies.append(trio)
    total = jnp.zeros((8, cols), jnp.float32)
    for part in range(parts):
        for copy in copies[part]:
            copy.wait()
        for c in range(part * size, (part + 1) * size):
            field = own_ref[c]
            shifted = DUAL_STEP * gain_ref[c] * field - DUAL_STEP * dirty_ref[c]
            shifted_ref[c] = shifted
            square = shifted * shifted
            for q in range(rows // 8):
                total = total + square[8 * q : 8 * q + 8]
            pack_ref[c] = pack_rows(field, cols - BORDER)
    energy_ref[:8] = total


def prepare_kernel(
    margin_ref, seed_ref, after_ref, rows_ref, rows_t_ref, cols_ref,
    basis_ref, a_ref, at_ref, g_ref,
):
    rank, channels = seed_ref.shape
    eye = row_iota((channels, channels)) == lane_iota((channels, channels))
    columns = []
    for r in range(rank):
        row = jnp.broadcast_to(seed_ref[r : r + 1, :], (channels, channels))
        column = jnp.sum(jnp.where(eye, row, 0.0), axis=1, keepdims=True)
        columns.append(jnp.broadcast_to(column, (channels, LANES)))
    for r in range(rank):
        vector = columns[r]
        vector = vector / jnp.sqrt(jnp.sum(vector * vector, axis=0, keepdims=True))
        basis_ref[r] = vector
        for later in range(r + 1, rank):
            along = jnp.sum(vector * columns[later], axis=0, keepdims=True)
            columns[later] = columns[later] - along * vector

    half, tall = rows_ref.shape[0] // LEVELS, rows_ref.shape[1]
    wide, double = cols_ref.shape[1:]
    cols = double // 2
    first_row = lax.axis_index("fy") == 0
    first_col = lax.axis_index("fx") == 0
    position = lane_iota((half, tall)) - BORDER
    position_t = row_iota((tall, half)) - BORDER
    a_parts, at_parts = [], []
    for level in range(LEVELS):
        width = jnp.where(first_row, 0, margin_ref[0, 0, level, 0])
        a_parts.append(jnp.where(position >= -width, rows_ref[level * half : (level + 1) * half], 0.0))
        at_parts.append(jnp.where(position_t >= -width, rows_t_ref[level], 0.0))
    a_high, a_low = terms(jnp.concatenate(a_parts, axis=0))
    a_ref[...] = jnp.concatenate([a_high, a_high, a_low], axis=1)
    at_pairs = [terms(part) for part in at_parts]
    at_ref[...] = jnp.concatenate(
        [pair[0] for pair in at_pairs] * 2 + [pair[1] for pair in at_pairs], axis=1
    )
    at = row_iota((wide, double))
    for level in range(LEVELS):
        width = jnp.where(first_col, 0, margin_ref[0, 0, level, 1])
        g = jnp.where((at < cols) | (at >= cols + BORDER - width), cols_ref[level], 0.0)
        g_high, g_low = terms(g)
        g_ref[level, 0] = g_high
        g_ref[level, 1] = g_low


def dot_t(a, b):
    return lax.dot_general(a, b, (((1,), (1,)), ((), ())), preferred_element_type=jnp.float32)


def bank_kernel(
    own_ref, corner_ref, left_ref, above_ref, a_ref, at_ref, g_ref, after_ref,
    own_out, above_out, left_out, corner_out, z_high, z_low, u_high, u_low,
):
    channels, rows, cols = own_out.shape
    wide = cols + LANES
    half = 2 * rows
    size = channels // 4
    groups = rows // 8

    for c in range(channels):
        upper = jnp.concatenate([above_ref[c], unpack_rows(corner_ref[c], 0, groups)], axis=1)
        lower = jnp.concatenate([own_ref[c], unpack_rows(left_ref[c], 0, groups)], axis=1)
        e_high, e_low = terms(jnp.concatenate([upper, lower], axis=0))
        z = dot(a_ref[...], jnp.concatenate([e_high, e_low, e_high], axis=0))
        part_high, part_low = terms(z)
        for level in range(LEVELS):
            z_high[level, c] = part_high[level * half : (level + 1) * half]
            z_low[level, c] = part_low[level * half : (level + 1) * half]

    low_rows = row_iota((half, 2 * cols)) < rows
    low_cols = lane_iota((half, 2 * cols)) < cols
    bound = jnp.where(low_rows & low_cols, 0.0, CLIP_LEVEL / BAND_STEP)
    for level in range(LEVELS):
        g_high, g_low = g_ref[level, 0], g_ref[level, 1]
        for start in range(0, channels, size):
            span = slice(start, start + size)
            zh = z_high[level, span].reshape(size * half, wide)
            zl = z_low[level, span].reshape(size * half, wide)
            coef = dot(jnp.concatenate([zh, zl, zh], axis=1), jnp.concatenate([g_high, g_high, g_low], axis=0))
            coef = coef.reshape(size, half, 2 * cols)
            coef = jnp.minimum(jnp.maximum(coef, -bound), bound).reshape(size * half, 2 * cols)
            t_high, t_low = terms(coef)
            u = dot_t(
                jnp.concatenate([t_high, t_low, t_high], axis=1),
                jnp.concatenate([g_high, g_high, g_low], axis=1),
            )
            part_high, part_low = terms(u)
            u_high[level, span] = part_high.reshape(size, half, wide)
            u_low[level, span] = part_low.reshape(size, half, wide)

    for c in range(channels):
        highs = [u_high[level, c] for level in range(LEVELS)]
        lows = [u_low[level, c] for level in range(LEVELS)]
        back = dot(at_ref[...], jnp.concatenate(highs + lows + highs, axis=0))
        above_out[BORDER * c : BORDER * (c + 1)] = back[:BORDER, :cols]
        own_out[c] = back[BORDER:, :cols]
        corner_out[8 * c : 8 * (c + 1)] = pack_rows(back[:BORDER, cols:], 0)
        left_out[8 * c : 8 * (c + 1)] = pack_rows(back[BORDER:, cols:], 0)


def begin_kernel(own_ref, shifted_ref, gain_ref, basis_ref, part_ref, after_ref, plain_ref, scaled_ref):
    channels, rows, cols = own_ref.shape
    rank = basis_ref.shape[0]
    plain = [jnp.zeros((rows, cols), jnp.float32) for r in range(rank)]
    scaled = [jnp.zeros((rows, cols), jnp.float32) for r in range(rank)]
    for c in range(channels):
        first = own_ref[c] - (PRIMAL_STEP * WEIGHT * BAND_STEP) * part_ref[c]
        second = PRIMAL_STEP * gain_ref[c] * shifted_ref[c]
        for r in range(rank):
            plain[r] = plain[r] + basis_ref[r, c : c + 1, :] * first
            scaled[r] = scaled[r] + basis_ref[r, c : c + 1, :] * second
    for r in range(rank):
        plain_ref[r] = plain[r]
        scaled_ref[r] = scaled[r]


def last_kernel(
    radius, shifted_ref, basis_ref, energy_ref, plain_ref, scaled_ref, below_ref, right_ref, corner_ref,
    image_hbm, dual_hbm, image_ref, dual_ref, sems,
):
    channels, rows, cols = shifted_ref.shape
    parts = sems.shape[1]
    size = channels // parts
    copies = []

    def send(k, part):
        at = pl.ds(part * size, size)
        source, target = ((dual_ref, dual_hbm), (image_ref, image_hbm))[k]
        copies.append(pltpu.make_async_copy(source.at[at], target.at[at], sems.at[k, part]))
        copies[-1].start()

    rank = basis_ref.shape[0]
    groups = rows // 8
    energy = energy_ref[...]
    for ref in (below_ref, right_ref, corner_ref):
        energy = energy + ref[pl.ds(ref.shape[0] - 8, 8)]
    energy = jnp.sum(jnp.sum(energy, axis=0, keepdims=True), axis=1, keepdims=True)
    factor = jnp.maximum(0.0, 1.0 - DUAL_STEP * radius / jnp.sqrt(energy + NORM_EPS))
    factor = jnp.broadcast_to(factor, (rows, cols))
    edge = lane_iota((rows, cols)) >= cols - BORDER
    weights = [jnp.zeros((rows, cols), jnp.float32) for r in range(rank)]
    for c in range(channels):
        dual_ref[c] = factor * shifted_ref[c]
        if (c + 1) % size == 0:
            send(0, c // size)
    for c in range(channels):
        strip = right_ref[8 * c : 8 * (c + 1)] + corner_ref[8 * c : 8 * (c + 1)]
        strip = unpack_rows(strip, cols - BORDER, groups)
        prior = below_ref[BORDER * c : BORDER * (c + 1)] + jnp.where(edge, strip, 0.0)
        for r in range(rank):
            weights[r] = weights[r] + basis_ref[r, c : c + 1, :] * prior
    for r in range(rank):
        weights[r] = (plain_ref[r] - factor * scaled_ref[r]) - (PRIMAL_STEP * WEIGHT * BAND_STEP) * weights[r]
    for c in range(channels):
        total = basis_ref[0, c : c + 1, :] * weights[0]
        for r in range(1, rank):
            total = total + basis_ref[r, c : c + 1, :] * weights[r]
        image_ref[c] = jnp.maximum(total, 0.0)
        if (c + 1) % size == 0:
            send(1, c // size)
    for copy in copies:
        copy.wait()


def shift(axis_sizes, steps):
    return [
        (
            a * axis_sizes[1] + b,
            (a + steps[0]) % axis_sizes[0] * axis_sizes[1] + (b + steps[1]) % axis_sizes[1],
        )
        for a in range(axis_sizes[0])
        for b in range(axis_sizes[1])
    ]


def add_kernel(value_ref, arrived_ref, *refs):
    refs[-1][...] = value_ref[:8] + arrived_ref[:8]


def doubling():
    rounds = []
    for axis in ("fy", "fx"):
        step = lax.axis_size(axis) // 2
        while step > 1:
            rounds.append((axis, step))
            step //= 2
    return rounds


def partner(value, round_):
    axis, step = round_
    return lax.ppermute(value, axis, [(i, i ^ step) for i in range(lax.axis_size(axis))])


def stamp_kernel(value_ref, arrived_ref, above_in, left_in, corner_in, total_ref, above_ref, left_ref, corner_ref):
    total = value_ref[...] + arrived_ref[...]
    total_ref[...] = total
    for ref in (above_ref, left_ref, corner_ref):
        ref[pl.ds(ref.shape[0] - 8, 8)] = total


def added(value, arrived, *after):
    return pl.pallas_call(
        add_kernel,
        out_shape=jax.ShapeDtypeStruct((8, value.shape[1]), value.dtype),
        in_specs=[pl.BlockSpec(memory_space=pltpu.VMEM)] * 2 + [pl.BlockSpec(memory_space=pl.ANY)] * len(after),
        out_specs=pl.BlockSpec(memory_space=pltpu.VMEM),
        compiler_params=pltpu.CompilerParams(vmem_limit_bytes=1024 * 1024),
        name="add",
    )(value, arrived, *after)


def per_device(start_image, dirty, sampling, basis_seed, margin):
    channels, rows, cols = start_image.shape
    rank = basis_seed.shape[1]
    sizes = (lax.axis_size("fy"), lax.axis_size("fx"))
    half = 2 * rows
    tall = rows + BORDER
    wide = cols + LANES
    radius = BALL_SCALE * math.sqrt(channels * rows * cols * sizes[0] * sizes[1])
    f32, bf16 = jnp.float32, jnp.bfloat16
    image_shape = jax.ShapeDtypeStruct((channels, rows, cols), f32)
    pack_shape = jax.ShapeDtypeStruct((channels, 8, LANES), f32)
    params = pltpu.CompilerParams(vmem_limit_bytes=16 * 1024 * 1024)
    vmem = pl.BlockSpec(memory_space=pltpu.VMEM)
    smem = pl.BlockSpec(memory_space=pltpu.SMEM)
    hbm = pl.BlockSpec(memory_space=pltpu.HBM)
    anywhere = pl.BlockSpec(memory_space=pl.ANY)

    def kept(value):
        return pltpu.with_memory_space_constraint(value, pltpu.HBM)

    def moved(value, steps):
        return lax.ppermute(value, ("fy", "fx"), shift(sizes, steps))

    above = moved(start_image, (1, 0))
    energy, pack, own, gain, shifted = pl.pallas_call(
        first_kernel,
        out_shape=(jax.ShapeDtypeStruct((8, cols), f32), pack_shape, image_shape, image_shape, image_shape),
        in_specs=[hbm] * 3,
        out_specs=(vmem,) * 5,
        scratch_shapes=[pltpu.VMEM((channels, rows, cols), f32), pltpu.SemaphoreType.DMA((1, 3))],
        compiler_params=params,
        name="first",
    )(kept(start_image), kept(dirty), kept(sampling))
    left = moved(pack, (0, 1))
    corner = moved(pack, (1, 1))

    rounds = doubling()
    energy = added(energy, partner(energy, rounds[0]))

    table = row_table(rows)
    table_t = np.ascontiguousarray(table.reshape(LEVELS, half, tall).transpose(0, 2, 1))
    basis, a, a_t, g = pl.pallas_call(
        prepare_kernel,
        out_shape=(
            jax.ShapeDtypeStruct((rank, channels, LANES), f32),
            jax.ShapeDtypeStruct((LEVELS * half, 3 * tall), bf16),
            jax.ShapeDtypeStruct((tall, 3 * LEVELS * half), bf16),
            jax.ShapeDtypeStruct((LEVELS, 2, wide, 2 * cols), bf16),
        ),
        in_specs=[smem, vmem, anywhere, vmem, vmem, vmem],
        out_specs=(vmem,) * 4,
        compiler_params=params,
        cost_estimate=AHEAD,
        name="prepare",
    )(margin, basis_seed.T, energy, table, table_t, col_table(cols))
    for round_ in rounds[1:-1]:
        energy = added(energy, partner(energy, round_), basis)
    arriving = partner(energy, rounds[-1])
    above_shape = jax.ShapeDtypeStruct((channels * BORDER + 8, cols), f32)
    strip_shape = jax.ShapeDtypeStruct((channels * 8 + 8, LANES), f32)
    own_part, *parts = pl.pallas_call(
        bank_kernel,
        out_shape=(image_shape, above_shape, strip_shape, strip_shape),
        in_specs=[vmem] * 7 + [anywhere],
        out_specs=(vmem,) * 4,
        scratch_shapes=[pltpu.VMEM((LEVELS, channels, half, wide), bf16)] * 4,
        compiler_params=params,
        name="bank",
    )(own, corner, left, above, a, a_t, g, energy)
    energy, *parts = pl.pallas_call(
        stamp_kernel,
        out_shape=(jax.ShapeDtypeStruct(energy.shape, f32), above_shape, strip_shape, strip_shape),
        in_specs=[vmem] * 5,
        out_specs=(vmem,) * 4,
        input_output_aliases={2: 1, 3: 2, 4: 3},
        compiler_params=pltpu.CompilerParams(vmem_limit_bytes=1024 * 1024),
        name="stamp",
    )(energy, arriving, *parts)
    below = moved(parts[0], (-1, 0))
    right = moved(parts[1], (0, -1))
    corner_back = moved(parts[2], (-1, -1))

    weight_shape = jax.ShapeDtypeStruct((rank, rows, cols), f32)
    plain, scaled = pl.pallas_call(
        begin_kernel,
        out_shape=(weight_shape, weight_shape),
        in_specs=[vmem] * 5 + [anywhere],
        out_specs=(vmem,) * 2,
        compiler_params=params,
        name="begin",
    )(own, shifted, gain, basis, own_part, energy)

    def last(*refs):
        last_kernel(radius, *refs)

    return pl.pallas_call(
        last,
        out_shape=(image_shape, image_shape),
        in_specs=[vmem] * 8,
        out_specs=(hbm, hbm),
        scratch_shapes=[
            pltpu.VMEM(image_shape.shape, f32),
            pltpu.VMEM(image_shape.shape, f32),
            pltpu.SemaphoreType.DMA((2, 2)),
        ],
        compiler_params=params,
        name="last",
    )(shifted, basis, energy, plain, scaled, below, right, corner_back)


def solution(mesh):
    return jax.shard_map(
        per_device,
        mesh=mesh,
        in_specs=(
            P(None, "fy", "fx"),
            P(None, "fy", "fx"),
            P(None, "fy", "fx"),
            P(),
            P("fy", "fx", None, None),
        ),
        out_specs=(P(None, "fy", "fx"), P(None, "fy", "fx")),
        check_vma=False,
    )
```
